32 devices in a mesh: py: 4 (over x, core), px: 8 (over z, y).
Axes of the slice: x: 2, y: 2, z: 4, core: 2. Of those that a mesh axis runs over, the one named last changes fastest.
Arguments:
- forcing: float32 [1024, 8, 1024], P('px', 'py')
- inv_density: float32 [1024, 8, 1024], P('px', 'py'), may hold values from 0.5 to 4
- stretch_x: float32 [1024], P('px'), may hold values from 0.5 to 2
- stretch_y: float32 [8], P('py'), may hold values from 0.5 to 2
- stretch_z: float32 [1024], replicated, may hold values from 0.5 to 2
- lines_z0: float32 [4, 256, 256], replicated
- lines_x0: float32 [4, 256, 256], replicated
- lines_z1: float32 [2, 256, 256], replicated
- lines_x1: float32 [2, 256, 256], replicated
- coarse_inverse: float32 [32, 32], P(('py', 'px')), as said below
Outputs:
- pressure_adjoint: float32 [1024, 8, 1024], P('px', 'py')
The draws below stay inside these ranges and needn't reach their ends.
Inputs may be any that keep to these rules, and one draw needn't show every extreme that they name: coarse_inverse is symmetric.
All inputs are finite; a program needn't handle non-finite values.
Results may differ from the reference program's by a relative error of at most 0.0001.
Values sent between devices are 32-bit elements; how exact they have to be, the bound alone decides.
A program may use at most 128 MiB of HBM per device.

```python
import math
import jax
import jax.numpy as jnp
from jax import lax

NX = 1024
NZ = 1024
B = 256
CYCLES = 1
NY = 8
COARSE = 32
N_PY = 4
N_PX = 8


def block_lines(key, count):
    first_key, second_key = jax.random.split(key)
    diag_part = jax.random.uniform(first_key, (count, B, B), jnp.float32, 0.45, 0.65)
    off_part = 0.12 * jax.random.normal(second_key, (count, B, B), jnp.float32) / math.sqrt(B)
    unit = jnp.eye(B, dtype=jnp.float32)
    return unit * diag_part + (1.0 - unit) * off_part


def draw_lines_z0(key, part):
    return block_lines(jax.random.fold_in(key, 11), NZ // B)


def draw_lines_x0(key, part):
    return block_lines(jax.random.fold_in(key, 12), NX // B)


def draw_lines_z1(key, part):
    return block_lines(jax.random.fold_in(key, 13), NZ // 2 // B)


def draw_lines_x1(key, part):
    return block_lines(jax.random.fold_in(key, 14), NX // 2 // B)


def draw_coarse_inverse(key, part):
    first_key, second_key = jax.random.split(jax.random.fold_in(key, 21))
    diag_part = jax.random.uniform(first_key, (COARSE, COARSE), jnp.float32, 1.0, 2.0)
    noise = jax.random.normal(second_key, (COARSE, COARSE), jnp.float32)
    mirrored = (noise + noise.T) * (0.35 / math.sqrt(COARSE))
    unit = jnp.eye(COARSE, dtype=jnp.float32)
    return unit * diag_part + (1.0 - unit) * mirrored


def draw_forcing(key, part):
    first_key, second_key = jax.random.split(jax.random.fold_in(key, 31))
    phases = jax.random.uniform(second_key, (3,), jnp.float32, 0.0, 2.0 * math.pi)
    along_x = (jnp.arange(NX, dtype=jnp.float32) + 0.5) / NX
    along_y = (jnp.arange(NY, dtype=jnp.float32) + 0.5) / NY
    along_z = (jnp.arange(NZ, dtype=jnp.float32) + 0.5) / NZ
    smooth = 1.2 * jnp.sin(2.0 * math.pi * along_x + phases[0])[:, None, None] * jnp.cos(2.0 * math.pi * along_y + phases[1])[None, :, None] * jnp.cos(math.pi * along_z + phases[2])[None, None, :]
    rough = jax.random.normal(first_key, (NX, NY, NZ), jnp.float32)
    return rough + smooth


def block_scale(key, dims, cuts, low, largest):
    loudness = 1.0
    for axis_at, parts in cuts:
        steps = jax.random.uniform(jax.random.fold_in(jax.random.fold_in(key, 6), axis_at), (parts,), jnp.float32, low / len(cuts), largest / len(cuts))
        loudness = loudness * jnp.repeat(jnp.exp(steps), dims[axis_at] // parts).reshape((-1,) + (1,) * (len(dims) - 1 - axis_at))
    return loudness


def setup_inputs(seed: int = 0) -> dict:
    splits = jax.random.split(jax.random.key(seed), 11)
    return {
        "forcing": draw_forcing(jax.random.fold_in(splits[10], 71), 0),
        "inv_density": jnp.clip(jnp.exp(math.log(4.0) - 2.0794415 * jax.random.uniform(splits[1], (NX, NY, NZ), jnp.float32) ** block_scale(splits[1], (NX, NY, NZ), ((0, 8), (1, 4)), -0.2, 0.2)), 0.5, 4.0),
        "stretch_x": jnp.clip(jnp.exp(math.log(2.0) - 1.3862944 * jax.random.uniform(splits[2], (NX,), jnp.float32) ** block_scale(splits[2], (NX,), ((0, 8),), -0.2, 0.2)), 0.5, 2.0),
        "stretch_y": jnp.clip(jnp.exp(math.log(2.0) - 1.3862944 * jax.random.uniform(splits[3], (NY,), jnp.float32) ** block_scale(splits[3], (NY,), ((0, 4),), -0.2, 0.2)), 0.5, 2.0),
        "stretch_z": jnp.clip(jnp.exp(jax.random.uniform(splits[4], (NZ,), jnp.float32, math.log(0.5), math.log(2.0))), 0.5, 2.0),
        "lines_z0": draw_lines_z0(jax.random.fold_in(splits[10], 71), 0),
        "lines_x0": draw_lines_x0(jax.random.fold_in(splits[10], 71), 0),
        "lines_z1": draw_lines_z1(jax.random.fold_in(splits[10], 71), 0),
        "lines_x1": draw_lines_x1(jax.random.fold_in(splits[10], 71), 0),
        "coarse_inverse": draw_coarse_inverse(jax.random.fold_in(splits[10], 71), 0),
    }


shift_term = 0.1
highest = lax.Precision.HIGHEST


def pad_axis(field, axis):
    widths = [(0, 0), (0, 0), (0, 0)]
    widths[axis] = (1, 1)
    return jnp.pad(field, widths)


def beside_sum(padded, axis):
    length = padded.shape[axis] - 2
    return lax.slice_in_dim(padded, 2, length + 2, axis=axis) + lax.slice_in_dim(padded, 0, length, axis=axis)


def operate(field, level):
    density, coef_x, coef_y, coef_z = level[0], level[1], level[2], level[3]
    twice = 2.0 * field
    near_x = beside_sum(pad_axis(field, 0), 0)
    near_y = beside_sum(pad_axis(field, 1), 1)
    near_z = beside_sum(pad_axis(field, 2), 2)
    stencil = coef_x[:, None, None] * (twice - near_x) + coef_y[None, :, None] * (twice - near_y) + coef_z[None, None, :] * (twice - near_z)
    return shift_term * field + density * stencil


def diagonal(density, coef_x, coef_y, coef_z):
    return shift_term + 2.0 * density * (coef_x[:, None, None] + coef_y[None, :, None] + coef_z[None, None, :])


def lines_along_z(field, blocks):
    first, second, third = field.shape
    count = blocks.shape[0]
    grouped = field.reshape(first * second, count, third // count)
    return jnp.einsum('nkb,kcb->nkc', grouped, blocks, precision=highest).reshape(first, second, third)


def lines_along_x(field, blocks):
    first, second, third = field.shape
    count = blocks.shape[0]
    grouped = field.reshape(count, first // count, second * third)
    return jnp.einsum('kcb,kbn->kcn', blocks, grouped, precision=highest).reshape(first, second, third)


def sweep(iterate, rhs, level):
    residual = rhs - operate(iterate, level)
    iterate = iterate + lines_along_z(residual / level[4], level[5])
    residual = rhs - operate(iterate, level)
    return iterate + lines_along_x(residual / level[4], level[6])


def restrict_padded(padded, axis):
    length = padded.shape[axis] - 2

    def take(start):
        return lax.slice_in_dim(padded, start, start + length - 1, stride=2, axis=axis)

    return (take(0) + 3.0 * take(1) + 3.0 * take(2) + take(3)) * 0.125


def prolong_padded(padded, axis):
    length = padded.shape[axis] - 2
    lower = lax.slice_in_dim(padded, 0, length, axis=axis)
    middle = lax.slice_in_dim(padded, 1, length + 1, axis=axis)
    upper = lax.slice_in_dim(padded, 2, length + 2, axis=axis)
    even = (3.0 * middle + lower) * 0.25
    odd = (3.0 * middle + upper) * 0.25
    stacked = jnp.stack([even, odd], axis=axis + 1)
    shape = list(even.shape)
    shape[axis] = 2 * length
    return stacked.reshape(shape)


def halve(vector):
    return vector.reshape(-1, 2).sum(axis=1) * 0.125


def coarsen(density, coef_x, coef_y, coef_z):
    first, second, third = density.shape
    dense_one = density.reshape(first // 2, 2, second // 2, 2, third // 2, 2).mean(axis=(1, 3, 5))
    return dense_one, halve(coef_x), halve(coef_y), halve(coef_z)


def reference(forcing, inv_density, stretch_x, stretch_y, stretch_z, lines_z0, lines_x0, lines_z1, lines_x1, coarse_inverse):
    fine = (inv_density, stretch_x, stretch_y, stretch_z, diagonal(inv_density, stretch_x, stretch_y, stretch_z), lines_z0, lines_x0)
    dense_one, coef_x1, coef_y1, coef_z1 = coarsen(inv_density, stretch_x, stretch_y, stretch_z)
    middle = (dense_one, coef_x1, coef_y1, coef_z1, diagonal(dense_one, coef_x1, coef_y1, coef_z1), lines_z1, lines_x1)
    iterate = jnp.zeros_like(forcing)
    for cycle in range(CYCLES):
        iterate = sweep(iterate, forcing, fine)
        residual = forcing - operate(iterate, fine)
        right_one = restrict_padded(pad_axis(residual, 0), 0)
        right_one = restrict_padded(pad_axis(right_one, 1), 1)
        right_one = restrict_padded(pad_axis(right_one, 2), 2)
        level_one = sweep(jnp.zeros_like(right_one), right_one, middle)
        residual_one = right_one - operate(level_one, middle)
        size_x, size_y, size_z = residual_one.shape
        means = residual_one.reshape(N_PX, size_x // N_PX, N_PY, size_y // N_PY, size_z).mean(axis=(1, 3, 4))
        values = means.T.reshape(-1)
        correction = jnp.dot(coarse_inverse, values, precision=highest)
        spread = correction.reshape(N_PY, N_PX).T
        spread = jnp.repeat(jnp.repeat(spread, size_x // N_PX, axis=0), size_y // N_PY, axis=1)
        level_one = level_one + spread[:, :, None]
        level_one = sweep(level_one, right_one, middle)
        raised = prolong_padded(pad_axis(level_one, 0), 0)
        raised = prolong_padded(pad_axis(raised, 1), 1)
        raised = prolong_padded(pad_axis(raised, 2), 2)
        iterate = iterate + raised
        iterate = sweep(iterate, forcing, fine)
    return iterate
```

```python
import functools

import jax
import jax.numpy as jnp
from jax import lax
from jax.experimental import pallas as pl
from jax.experimental.pallas import tpu as pltpu
from jax.sharding import PartitionSpec as P

f32 = jnp.float32
bf16 = jnp.bfloat16
MESH = pl.DeviceIdType.MESH
shift_term = 0.1
H = 8


def split(a):
    hi = a.astype(bf16)
    return hi, (a - hi.astype(f32)).astype(bf16)


def mm(a, b, transposed=False):
    dims = (((1,), (1 if transposed else 0,)), ((), ()))
    return lax.dot_general(a, b, dims, preferred_element_type=f32)


def mm3(a, b, transposed=False):
    (ah, al), (bh, bl) = a, b
    return mm(ah, bh, transposed) + (mm(ah, bl, transposed) + mm(al, bh, transposed))


def weights(shape, fine_dim, fine_pad, coarse_pad, inner, outer):
    fine = lax.broadcasted_iota(jnp.int32, shape, fine_dim) - fine_pad
    coarse = lax.broadcasted_iota(jnp.int32, shape, 1 - fine_dim) - coarse_pad
    d = fine - 2 * coarse
    near = jnp.where((d == 0) | (d == 1), inner, 0.0)
    if outer:
        near = jnp.where((d == -1) | (d == 2), outer, near)
    return near.astype(bf16)


def left_mul(m, v):
    hi, lo = split(v)
    return mm(m, hi) + mm(m, lo)


def right_mul(v, m):
    hi, lo = split(v)
    return mm(hi, m) + mm(lo, m)


def kernel(
    dims,
    f_in, rho_in, sx_ref, sy_ref, sz_ref, lz0_ref, lx0_in, lz1_ref, lx1_in, c_ref,
    out_ref,
    F, RHO, RD, UA, UB, UC, UD, W, W2, R0, T1, F1, RHO1, RD1,
    M1, M2, MP, M3, M4, V, V2, G1, G2, CB, CX, CX1, CZ1, LX0, LX1, OUT,
    ss, rs, ls,
):
    n, ny, nz, B, npx, npy = dims
    n1, ny1, nz1 = n // 2, ny // 2, nz // 2
    nk, nk1 = nz // B, nz1 // B
    g, g1 = B // n, B // n1
    i, j = lax.axis_index("px"), lax.axis_index("py")
    has_xm, has_xp = i > 0, i < npx - 1
    has_ym, has_yp = j > 0, j < npy - 1
    xm, xp = lax.rem(i + npx - 1, npx), lax.rem(i + 1, npx)
    ym, yp = lax.rem(j + npy - 1, npy), lax.rem(j + 1, npy)

    loads = []
    for y in range(ny):
        loads.append(pltpu.make_async_copy(f_in.at[:, y, :], F.at[y], ls.at[2 * y]))
        loads.append(pltpu.make_async_copy(rho_in.at[:, y, :], RHO.at[y], ls.at[2 * y + 1]))
    at0 = pl.multiple_of(lax.rem(i, g) * n, n)
    at1 = pl.multiple_of(lax.rem(i, g1) * n1, n1)
    loads.append(pltpu.make_async_copy(lx0_in.at[i // g, pl.ds(at0, n), :], LX0, ls.at[2 * ny]))
    loads.append(pltpu.make_async_copy(lx1_in.at[i // g1, pl.ds(at1, n1), :], LX1, ls.at[2 * ny + 1]))
    for load in loads:
        load.start()

    for ref in (UA, UB, UD, R0, M1, M2, M3, M4):
        rows = ref.shape[1]

        @pl.when(jnp.logical_not(has_xm))
        def _(ref=ref):
            ref[:, 0:H, :] = jnp.zeros((ref.shape[0], H, ref.shape[2]), f32)

        @pl.when(jnp.logical_not(has_xp))
        def _(ref=ref, rows=rows):
            ref[:, rows - H:rows, :] = jnp.zeros((ref.shape[0], H, ref.shape[2]), f32)

    for ref in (UA, UB, UD, T1, M1, M2, M3, M4):
        planes = ref.shape[0]

        @pl.when(jnp.logical_not(has_ym))
        def _(ref=ref):
            ref[0] = jnp.zeros(ref.shape[1:], f32)

        @pl.when(jnp.logical_not(has_yp))
        def _(ref=ref, planes=planes):
            ref[planes - 1] = jnp.zeros(ref.shape[1:], f32)

    count = c_ref.shape[1]
    CB[...] = jnp.zeros(CB.shape, f32)
    CB[0, :, 0:count] = jnp.broadcast_to(c_ref[...], (8, count))

    barrier = pltpu.get_barrier_semaphore()
    for s in range(1, npx):
        pl.semaphore_signal(barrier, inc=1, device_id={"px": lax.rem(i + s, npx), "py": j}, device_id_type=MESH)
    for s in range(1, npy):
        pl.semaphore_signal(barrier, inc=1, device_id={"px": i, "py": lax.rem(j + s, npy)}, device_id_type=MESH)
    for to_x in (xm, xp):
        for to_y in (ym, yp):
            pl.semaphore_signal(barrier, inc=1, device_id={"px": to_x, "py": to_y}, device_id_type=MESH)

    pending = []

    def push(src, dst, to_x, to_y, sends=None, receives=None):
        at = len(pending)
        copy = pltpu.make_async_remote_copy(
            src_ref=src, dst_ref=dst, send_sem=ss.at[at], recv_sem=rs.at[at],
            device_id={"px": to_x, "py": to_y}, device_id_type=MESH,
        )
        if sends is None:
            copy.start()
        else:
            pl.when(sends)(copy.start)
        pending.append((sends, copy))
        return receives, copy

    def arrive(handles):
        for receives, copy in handles:
            if receives is None:
                copy.wait_recv()
            else:
                pl.when(receives)(copy.wait_recv)

    def halo_x(ref, planes, rows, zs):
        a, b = planes
        return [
            push(ref.at[a:b, rows:rows + H, zs], ref.at[a:b, 0:H, zs], xp, j, has_xp, has_xm),
            push(ref.at[a:b, H:2 * H, zs], ref.at[a:b, rows + H:rows + 2 * H, zs], xm, j, has_xm, has_xp),
        ]

    def halo_y(ref, planes, r, zs):
        return [
            push(ref.at[planes, r, zs], ref.at[0, r, zs], i, yp, has_yp, has_ym),
            push(ref.at[1, r, zs], ref.at[planes + 1, r, zs], i, ym, has_ym, has_yp),
        ]

    def halo(ref, planes, rows, zs):
        return halo_y(ref, planes, slice(H, H + rows), zs) + halo_x(ref, (1, planes + 1), rows, zs)

    def halo_corners(ref, planes, rows):
        both = jnp.logical_and
        low, high = slice(0, H), slice(rows + H, rows + 2 * H)
        first, last = slice(H, 2 * H), slice(rows, rows + H)
        return [
            push(ref.at[planes, last, :], ref.at[0, low, :], xp, yp, both(has_xp, has_yp), both(has_xm, has_ym)),
            push(ref.at[1, last, :], ref.at[planes + 1, low, :], xp, ym, both(has_xp, has_ym), both(has_xm, has_yp)),
            push(ref.at[planes, first, :], ref.at[0, high, :], xm, yp, both(has_xm, has_yp), both(has_xp, has_ym)),
            push(ref.at[1, first, :], ref.at[planes + 1, high, :], xm, ym, both(has_xm, has_ym), both(has_xp, has_yp)),
        ]

    def to_block(ref, at, rows, peers, zs):
        here = lax.rem(i, peers)
        base = i - here
        mine = ref.at[:, pl.ds(at, rows), zs]
        return [push(mine, mine, base + lax.rem(here + s, peers), j) for s in range(1, peers)]

    def residual(rhs, ref, rho, cx, cys, cz, y, k):
        rows = rhs.shape[1]
        lo = k * B
        zs = slice(lo, lo + B)
        own = slice(H, H + rows)
        c = ref[y + 1, own, zs]
        near_x = ref[y + 1, H - 1:H - 1 + rows, zs] + ref[y + 1, H + 1:H + 1 + rows, zs]
        near_y = ref[y, own, zs] + ref[y + 2, own, zs]
        blank = jnp.zeros((rows, 128), f32)
        left = ref[y + 1, own, lo - 128:lo] if lo > 0 else blank
        right = ref[y + 1, own, lo + B:lo + B + 128] if lo + B < ref.shape[2] else blank
        wide = jnp.concatenate([left, c, right], axis=1)
        near_z = (pltpu.roll(wide, 1, 1) + pltpu.roll(wide, B + 255, 1))[:, 128:128 + B]
        twice = 2.0 * c
        stencil = cx[...] * (twice - near_x) + cys[y] * (twice - near_y) + cz[0:1, zs] * (twice - near_z)
        return rhs[y, :, zs] - (shift_term * c + rho[y, :, zs] * stencil)

    def inverse_diagonal(rho, cx, cys, cz, y, k):
        zs = slice(k * B, k * B + B)
        return 1.0 / (shift_term + 2.0 * rho[y, :, zs] * (cx[...] + cys[y] + cz[0:1, zs]))

    square = (n, n)
    diag = lax.broadcasted_iota(jnp.int32, square, 0) == lax.broadcasted_iota(jnp.int32, square, 1)
    column = jnp.sum(jnp.where(diag, jnp.broadcast_to(sx_ref[...], square), 0.0), axis=1, keepdims=True)
    CX[...] = jnp.broadcast_to(column, (n, B))
    cy = [sy_ref[y] for y in range(ny)]
    cy1 = [(cy[2 * y] + cy[2 * y + 1]) * 0.125 for y in range(ny1)]

    for load in loads:
        load.wait()
    pl.semaphore_wait(barrier, npx + npy + 2)

    whole = slice(None)
    neighbours = [
        push(CB.at[0], CB.at[1], xp, j, has_xp, has_xm),
        push(CB.at[0], CB.at[2], xm, j, has_xm, has_xp),
        push(CB.at[0], CB.at[3], i, yp, has_yp, has_ym),
        push(CB.at[0], CB.at[4], i, ym, has_ym, has_yp),
    ]

    def smooth_z(values, block, planes, rows):
        w = jnp.concatenate(values, axis=0)
        z = mm3(split(w), split(block), True)
        return [z[y * rows:(y + 1) * rows] for y in range(planes)]

    own = slice(H, H + n)
    halos = []
    for k in range(nk):
        zs = slice(k * B, k * B + B)
        scaled = []
        for y in range(ny):
            rd = inverse_diagonal(RHO, CX, cy, sz_ref, y, k)
            RD[y, :, zs] = rd
            scaled.append(F[y, :, zs] * rd)
        solved = smooth_z(scaled, lz0_ref[k], ny, n)
        for y in range(ny):
            UA[y + 1, own, zs] = solved[y]
        halos.append(halo(UA, ny, n, zs))

    def exchange_fine(ref, halos, target):
        blocks = []
        for k in range(nk):
            zs = slice(k * B, k * B + B)
            arrive(halos[k])
            for y in range(ny):
                r = residual(F, ref, RHO, CX, cy, sz_ref, y, k)
                target[y, pl.ds(at0, n), zs] = r * RD[y, :, zs]
            blocks.append(to_block(target, at0, n, g, zs))
        return blocks

    blocks = exchange_fine(UA, halos, W)

    restrict_x = weights((n1, n + 2 * H), 1, H, 0, 0.375, 0.125)
    restrict_z = weights((nz, nz1), 0, 0, 0, 0.375, 0.125)
    mean_x = weights((n1, n), 1, 0, 0, 0.5, 0.0)
    mean_z = weights((nz, nz1), 0, 0, 0, 0.5, 0.0)
    CX1[...] = left_mul(mean_x, CX[...]) * 0.25
    CZ1[...] = right_mul(jnp.broadcast_to(sz_ref[...], (8, nz)), mean_z) * 0.25
    for y in range(ny1):
        pair = (RHO[2 * y] + RHO[2 * y + 1]) * 0.5
        RHO1[y] = right_mul(left_mul(mean_x, pair), mean_z)
    for y in range(ny1):
        for k in range(nk1):
            RD1[y, :, k * B:k * B + B] = inverse_diagonal(RHO1, CX1, cy1, CZ1, y, k)

    lx0 = split(LX0[...])
    halos = []
    for k in range(nk):
        zs = slice(k * B, k * B + B)
        arrive(blocks[k])
        for y in range(ny):
            UB[y + 1, own, zs] = UA[y + 1, own, zs] + mm3(lx0, split(W[y, :, zs]))
        halos.append(halo(UB, ny, n, zs))

    for k in range(nk):
        zs = slice(k * B, k * B + B)
        arrive(halos[k])
        for y in range(ny):
            R0[y, own, zs] = residual(F, UB, RHO, CX, cy, sz_ref, y, k)
    arrive(halo_x(R0, (0, ny), n, whole))
    for y in range(ny):
        T1[y + 1] = right_mul(left_mul(restrict_x, R0[y]), restrict_z)
    arrive(halo_y(T1, ny, whole, whole))
    for y in range(ny1):
        a = 2 * y
        F1[y] = (T1[a] + 3.0 * T1[a + 1] + 3.0 * T1[a + 2] + T1[a + 3]) * 0.125

    own1 = slice(H, H + n1)

    def middle_z(ref, before, rhs):
        for k in range(nk1):
            zs = slice(k * B, k * B + B)
            solved = smooth_z([r * RD1[y, :, zs] for y, r in enumerate(rhs(k))], lz1_ref[k], ny1, n1)
            for y in range(ny1):
                ref[y + 1, own1, zs] = solved[y] if before is None else before[y + 1, own1, zs] + solved[y]
        return halo(ref, ny1, n1, whole)

    def middle_x(ref, target, result):
        for k in range(nk1):
            zs = slice(k * B, k * B + B)
            for y in range(ny1):
                r = residual(F1, ref, RHO1, CX1, cy1, CZ1, y, k)
                target[y, pl.ds(at1, n1), zs] = r * RD1[y, :, zs]
        arrive(to_block(target, at1, n1, g1, whole))
        lx1 = split(LX1[...])
        for y in range(ny1):
            result[y + 1, own1, :] = ref[y + 1, own1, :] + mm3(lx1, split(target[y]))

    arrive(middle_z(M1, None, lambda k: [F1[y, :, k * B:k * B + B] for y in range(ny1)]))
    middle_x(M1, V, M2)
    arrive(halo(M2, ny1, n1, whole))

    total = jnp.zeros((1, B), f32)
    for y in range(ny1):
        for k in range(nk1):
            r = residual(F1, M2, RHO1, CX1, cy1, CZ1, y, k)
            total = total + jnp.sum(r, axis=0, keepdims=True)
    mean = jnp.sum(total, axis=1, keepdims=True) * (1.0 / (ny1 * n1 * nz1))
    lane = lax.broadcasted_iota(jnp.int32, CB.shape[1:], 1)
    G1[i] = jnp.where(lane == j * npx + i, mean, 0.0)
    arrive([push(G1.at[i], G1.at[i], lax.rem(i + s, npx), j) for s in range(1, npx)])
    G2[j] = jnp.sum(G1[...], axis=0)
    arrive([push(G2.at[j], G2.at[j], i, lax.rem(j + s, npy)) for s in range(1, npy)])
    means = jnp.sum(G2[...], axis=0)[0:1]
    arrive(neighbours)
    e = [jnp.sum(CB[s][0:1] * means, axis=1, keepdims=True) for s in range(5)]
    MP[1:ny1 + 1, own1, :] = M2[1:ny1 + 1, own1, :] + e[0]
    MP[1:ny1 + 1, 0:H, :] = M2[1:ny1 + 1, 0:H, :] + e[1]
    MP[1:ny1 + 1, n1 + H:n1 + 2 * H, :] = M2[1:ny1 + 1, n1 + H:n1 + 2 * H, :] + e[2]
    MP[0, own1, :] = M2[0, own1, :] + e[3]
    MP[ny1 + 1, own1, :] = M2[ny1 + 1, own1, :] + e[4]

    arrive(middle_z(M3, MP, lambda k: [residual(F1, MP, RHO1, CX1, cy1, CZ1, y, k) for y in range(ny1)]))
    middle_x(M3, V2, M4)
    handles = halo(M4, ny1, n1, whole) + halo_corners(M4, ny1, n1)
    raise_x = weights((n + 2 * H, n1 + 2 * H), 0, H, H, 0.75, 0.25)
    raise_z = weights((nz1, nz), 1, 0, 0, 0.75, 0.25)
    arrive(handles)

    raised = [left_mul(raise_x, right_mul(M4[y], raise_z)) for y in range(ny1 + 2)]
    row = lax.broadcasted_iota(jnp.int32, (n + 2 * H, 1), 0)
    inside = jnp.logical_and(jnp.logical_or(row >= H, has_xm), jnp.logical_or(row < n + H, has_xp))
    for y in range(ny + 2):
        near = (y - 1) // 2 + 1
        other = near - 1 if (y - 1) % 2 == 0 else near + 1
        c = (3.0 * raised[near] + raised[other]) * 0.25
        if y == 0:
            UC[0, own, :] = jnp.where(has_ym, UB[0, own, :] + c[own], 0.0)
        elif y == ny + 1:
            UC[y, own, :] = jnp.where(has_yp, UB[y, own, :] + c[own], 0.0)
        else:
            UC[y] = jnp.where(inside, UB[y] + c, 0.0)

    halos = []
    for k in range(nk):
        zs = slice(k * B, k * B + B)
        scaled = [residual(F, UC, RHO, CX, cy, sz_ref, y, k) * RD[y, :, zs] for y in range(ny)]
        solved = smooth_z(scaled, lz0_ref[k], ny, n)
        for y in range(ny):
            UD[y + 1, own, zs] = UC[y + 1, own, zs] + solved[y]
        halos.append(halo(UD, ny, n, zs))
    blocks = exchange_fine(UD, halos, W2)
    lx0 = split(LX0[...])
    for k in range(nk):
        zs = slice(k * B, k * B + B)
        arrive(blocks[k])
        for y in range(ny):
            OUT[y, :, zs] = UD[y + 1, own, zs] + mm3(lx0, split(W2[y, :, zs]))
    stores = [pltpu.make_async_copy(OUT.at[y], out_ref.at[:, y, :], ls.at[y]) for y in range(ny)]
    for store in stores:
        store.start()
    for sends, copy in pending:
        if sends is None:
            copy.wait_send()
        else:
            pl.when(sends)(copy.wait_send)
    for store in stores:
        store.wait()


def per_device(npx, npy, f, rho, sx, sy, sz, lz0, lx0, lz1, lx1, c):
    n, ny, nz = f.shape
    B = lz0.shape[-1]
    n1, ny1, nz1 = n // 2, ny // 2, nz // 2
    g, g1, nk = B // n, B // n1, nz // B
    lanes = -(-c.shape[1] // 128) * 128
    fine = pltpu.VMEM((ny, n, nz), f32)
    padded = pltpu.VMEM((ny + 2, n + 2 * H, nz), f32)
    coarse = pltpu.VMEM((ny1, n1, nz1), f32)
    coarse_padded = pltpu.VMEM((ny1 + 2, n1 + 2 * H, nz1), f32)
    copies = 4 + 12 * nk + 2 * nk * (g - 1) + 4 + 4 * 4 + 4 + 2 * (g1 - 1) + npx + npy - 2
    anywhere = pl.BlockSpec(memory_space=pl.ANY)
    vmem = pl.BlockSpec(memory_space=pltpu.VMEM)
    smem = pl.BlockSpec(memory_space=pltpu.SMEM)
    return pl.pallas_call(
        functools.partial(kernel, (n, ny, nz, B, npx, npy)),
        out_shape=jax.ShapeDtypeStruct(f.shape, f32),
        in_specs=[anywhere, anywhere, vmem, smem, vmem, vmem, anywhere, vmem, anywhere, vmem],
        out_specs=anywhere,
        scratch_shapes=[
            fine, fine, fine, padded, padded, padded, padded,
            pltpu.VMEM((ny, B, nz), f32), pltpu.VMEM((ny, B, nz), f32),
            pltpu.VMEM((ny, n + 2 * H, nz), f32), pltpu.VMEM((ny + 2, n1, nz1), f32),
            coarse, coarse, coarse,
            coarse_padded, coarse_padded, coarse_padded, coarse_padded, coarse_padded,
            pltpu.VMEM((ny1, B, nz1), f32), pltpu.VMEM((ny1, B, nz1), f32),
            pltpu.VMEM((npx, 8, lanes), f32), pltpu.VMEM((npy, 8, lanes), f32), pltpu.VMEM((5, 8, lanes), f32),
            pltpu.VMEM((n, B), f32), pltpu.VMEM((n1, B), f32), pltpu.VMEM((8, nz1), f32),
            pltpu.VMEM((n, B), f32), pltpu.VMEM((n1, B), f32), fine,
            pltpu.SemaphoreType.DMA((copies,)), pltpu.SemaphoreType.DMA((copies,)),
            pltpu.SemaphoreType.DMA((2 * ny + 2,)),
        ],
        compiler_params=pltpu.CompilerParams(
            collective_id=0, has_side_effects=True, vmem_limit_bytes=56 * 1024 * 1024
        ),
    )(f, rho, sx.reshape(1, n), sy, sz.reshape(1, nz), lz0, lx0, lz1, lx1, c)


def solution(mesh):
    placed = (
        P("px", "py", None), P("px", "py", None), P("px"), P("py"),
        P(), P(), P(), P(), P(), P(("py", "px"), None),
    )
    body = functools.partial(per_device, mesh.shape["px"], mesh.shape["py"])
    return jax.shard_map(
        body, mesh=mesh, in_specs=placed, out_specs=P("px", "py", None), check_vma=False
    )
```

```python
import functools

import jax
import jax.numpy as jnp
from jax import lax
from jax.experimental import pallas as pl
from jax.experimental.pallas import tpu as pltpu
from jax.sharding import PartitionSpec as P

f32 = jnp.float32
bf16 = jnp.bfloat16
MESH = pl.DeviceIdType.MESH
shift_term = 0.1
H = 8


def split(a):
    hi = a.astype(bf16)
    return hi, (a - hi.astype(f32)).astype(bf16)


def mm(a, b, transposed=False):
    dims = (((1,), (1 if transposed else 0,)), ((), ()))
    return lax.dot_general(a, b, dims, preferred_element_type=f32)


def mm3(a, b, transposed=False):
    (ah, al), (bh, bl) = a, b
    return mm(ah, bh, transposed) + (mm(ah, bl, transposed) + mm(al, bh, transposed))


def weights(shape, fine_dim, fine_pad, coarse_pad, inner, outer):
    fine = lax.broadcasted_iota(jnp.int32, shape, fine_dim) - fine_pad
    coarse = lax.broadcasted_iota(jnp.int32, shape, 1 - fine_dim) - coarse_pad
    d = fine - 2 * coarse
    near = jnp.where((d == 0) | (d == 1), inner, 0.0)
    if outer:
        near = jnp.where((d == -1) | (d == 2), outer, near)
    return near.astype(bf16)


def left_mul(m, v):
    hi, lo = split(v)
    return mm(m, hi) + mm(m, lo)


def right_mul(v, m):
    hi, lo = split(v)
    return mm(hi, m) + mm(lo, m)


def kernel(
    dims,
    f_in, rho_in, sx_ref, sy_ref, sz_ref, lz0_in, lx0_in, lz1_in, lx1_in, c_ref,
    out_ref,
    F, RHO, RD, UA, UB, UC, UD, W, W2, R0, TX, T1, F1, RHO1, RD1,
    M1, M2, MP, M3, M4, V, V2, G1, G2, CB, CX, CX1, CZ1, LZ0, LZ1, LX0, LX1, OUT,
    ss, rs, ls,
):
    n, ny, nz, B, npx, npy = dims
    n1, ny1, nz1 = n // 2, ny // 2, nz // 2
    nk, nk1 = nz // B, nz1 // B
    g, g1 = B // n, B // n1
    i, j = lax.axis_index("px"), lax.axis_index("py")
    has_xm, has_xp = i > 0, i < npx - 1
    has_ym, has_yp = j > 0, j < npy - 1
    xm, xp = lax.rem(i + npx - 1, npx), lax.rem(i + 1, npx)
    ym, yp = lax.rem(j + npy - 1, npy), lax.rem(j + 1, npy)

    loads = []

    def load(src, dst):
        copy = pltpu.make_async_copy(src, dst, ls.at[len(loads)])
        copy.start()
        loads.append(copy)
        return copy

    half = B // 2
    cols = [slice(k * B, k * B + B) for k in range(nk)]
    parts = []
    for k in range(nk):
        part = [load(lz0_in.at[k], LZ0.at[k])]
        for y in range(ny):
            part.append(load(f_in.at[:, y, cols[k]], F.at[y, :, cols[k]]))
            part.append(load(rho_in.at[:, y, cols[k]], RHO.at[y, :, cols[k]]))
        parts.append(part)
    at0 = pl.multiple_of(lax.rem(i, g) * n, n)
    at1 = pl.multiple_of(lax.rem(i, g1) * n1, n1)
    late = [
        load(lx0_in.at[i // g, pl.ds(at0, n), :], LX0),
        load(lx1_in.at[i // g1, pl.ds(at1, n1), :], LX1),
        load(lz1_in, LZ1),
    ]

    for ref in (UA, UB, UD, R0, M1, M2, M3, M4):
        rows = ref.shape[1]

        @pl.when(jnp.logical_not(has_xm))
        def _(ref=ref):
            ref[:, 0:H, :] = jnp.zeros((ref.shape[0], H, ref.shape[2]), f32)

        @pl.when(jnp.logical_not(has_xp))
        def _(ref=ref, rows=rows):
            ref[:, rows - H:rows, :] = jnp.zeros((ref.shape[0], H, ref.shape[2]), f32)

    for ref in (UA, UB, UD, T1, M1, M2, M3, M4):
        planes = ref.shape[0]

        @pl.when(jnp.logical_not(has_ym))
        def _(ref=ref):
            ref[0] = jnp.zeros(ref.shape[1:], f32)

        @pl.when(jnp.logical_not(has_yp))
        def _(ref=ref, planes=planes):
            ref[planes - 1] = jnp.zeros(ref.shape[1:], f32)

    count = c_ref.shape[1]
    CB[...] = jnp.zeros(CB.shape, f32)
    CB[0, :, 0:count] = jnp.broadcast_to(c_ref[...], (8, count))

    barrier = pltpu.get_barrier_semaphore()
    for s in range(1, npx):
        pl.semaphore_signal(barrier, inc=1, device_id={"px": lax.rem(i + s, npx), "py": j}, device_id_type=MESH)
    for s in range(1, npy):
        pl.semaphore_signal(barrier, inc=1, device_id={"px": i, "py": lax.rem(j + s, npy)}, device_id_type=MESH)
    for to_x in (xm, xp):
        for to_y in (ym, yp):
            pl.semaphore_signal(barrier, inc=1, device_id={"px": to_x, "py": to_y}, device_id_type=MESH)

    pending = []

    def push(src, dst, to_x, to_y, sends=None, receives=None):
        at = len(pending)
        copy = pltpu.make_async_remote_copy(
            src_ref=src, dst_ref=dst, send_sem=ss.at[at], recv_sem=rs.at[at],
            device_id={"px": to_x, "py": to_y}, device_id_type=MESH,
        )
        if sends is None:
            copy.start()
        else:
            pl.when(sends)(copy.start)
        pending.append((sends, copy))
        return receives, copy

    def arrive(handles):
        for receives, copy in handles:
            if receives is None:
                copy.wait_recv()
            else:
                pl.when(receives)(copy.wait_recv)

    def halo_x(ref, planes, rows, zs):
        a, b = planes
        return [
            push(ref.at[a:b, rows:rows + H, zs], ref.at[a:b, 0:H, zs], xp, j, has_xp, has_xm),
            push(ref.at[a:b, H:2 * H, zs], ref.at[a:b, rows + H:rows + 2 * H, zs], xm, j, has_xm, has_xp),
        ]

    def halo_y(ref, planes, r, zs):
        return [
            push(ref.at[planes, r, zs], ref.at[0, r, zs], i, yp, has_yp, has_ym),
            push(ref.at[1, r, zs], ref.at[planes + 1, r, zs], i, ym, has_ym, has_yp),
        ]

    def halo(ref, planes, rows, zs):
        return halo_y(ref, planes, slice(H, H + rows), zs) + halo_x(ref, (1, planes + 1), rows, zs)

    def halo_corners(ref, planes, rows, zs):
        both = jnp.logical_and
        low, high = slice(0, H), slice(rows + H, rows + 2 * H)
        first, last = slice(H, 2 * H), slice(rows, rows + H)
        return [
            push(ref.at[planes, last, zs], ref.at[0, low, zs], xp, yp, both(has_xp, has_yp), both(has_xm, has_ym)),
            push(ref.at[1, last, zs], ref.at[planes + 1, low, zs], xp, ym, both(has_xp, has_ym), both(has_xm, has_yp)),
            push(ref.at[planes, first, zs], ref.at[0, high, zs], xm, yp, both(has_xm, has_yp), both(has_xp, has_ym)),
            push(ref.at[1, first, zs], ref.at[planes + 1, high, zs], xm, ym, both(has_xm, has_ym), both(has_xp, has_yp)),
        ]

    def to_block(ref, at, rows, peers, zs):
        here = lax.rem(i, peers)
        base = i - here
        mine = ref.at[:, pl.ds(at, rows), zs]
        return [push(mine, mine, base + lax.rem(here + s, peers), j) for s in range(1, peers)]

    def residual(rhs, ref, rho, cx, cys, cz, y, k):
        rows = rhs.shape[1]
        lo = k * B
        zs = slice(lo, lo + B)
        own = slice(H, H + rows)
        c = ref[y + 1, own, zs]
        near_x = ref[y + 1, H - 1:H - 1 + rows, zs] + ref[y + 1, H + 1:H + 1 + rows, zs]
        near_y = ref[y, own, zs] + ref[y + 2, own, zs]
        blank = jnp.zeros((rows, 128), f32)
        left = ref[y + 1, own, lo - 128:lo] if lo > 0 else blank
        right = ref[y + 1, own, lo + B:lo + B + 128] if lo + B < ref.shape[2] else blank
        wide = jnp.concatenate([left, c, right], axis=1)
        near_z = (pltpu.roll(wide, 1, 1) + pltpu.roll(wide, B + 255, 1))[:, 128:128 + B]
        twice = 2.0 * c
        stencil = cx[...] * (twice - near_x) + cys[y] * (twice - near_y) + cz[0:1, zs] * (twice - near_z)
        return rhs[y, :, zs] - (shift_term * c + rho[y, :, zs] * stencil)

    def inverse_diagonal(rho, cx, cys, cz, y, k):
        zs = slice(k * B, k * B + B)
        return 1.0 / (shift_term + 2.0 * rho[y, :, zs] * (cx[...] + cys[y] + cz[0:1, zs]))

    square = (n, n)
    diag = lax.broadcasted_iota(jnp.int32, square, 0) == lax.broadcasted_iota(jnp.int32, square, 1)
    column = jnp.sum(jnp.where(diag, jnp.broadcast_to(sx_ref[...], square), 0.0), axis=1, keepdims=True)
    CX[...] = jnp.broadcast_to(column, (n, B))
    cy = [sy_ref[y] for y in range(ny)]
    cy1 = [(cy[2 * y] + cy[2 * y + 1]) * 0.125 for y in range(ny1)]

    neighbours = []

    def enter():
        pl.semaphore_wait(barrier, npx + npy + 2)
        neighbours.extend([
            push(CB.at[0], CB.at[1], xp, j, has_xp, has_xm),
            push(CB.at[0], CB.at[2], xm, j, has_xm, has_xp),
            push(CB.at[0], CB.at[3], i, yp, has_yp, has_ym),
            push(CB.at[0], CB.at[4], i, ym, has_ym, has_yp),
        ])

    def smooth_z(values, block, planes, rows):
        w = jnp.concatenate(values, axis=0)
        z = mm3(split(w), split(block), True)
        return [z[y * rows:(y + 1) * rows] for y in range(planes)]

    def window(ref, y, k, width, side):
        lo = k * width
        parts = [ref[y, :, lo:lo + width]]
        blank = jnp.zeros((ref.shape[1], side), f32)
        parts.insert(0, ref[y, :, lo - side:lo] if lo > 0 else blank)
        parts.append(ref[y, :, lo + width:lo + width + side] if lo + width < ref.shape[2] else blank)
        return jnp.concatenate(parts, axis=1)

    own = slice(H, H + n)
    own1 = slice(H, H + n1)
    mean_x = weights((n1, n), 1, 0, 0, 0.5, 0.0)
    mean_z = weights((B, half), 0, 0, 0, 0.5, 0.0)

    def scaled_residual(ref, halos, target, blocks, k):
        arrive(halos[k])
        for y in range(ny):
            r = residual(F, ref, RHO, CX, cy, sz_ref, y, k)
            target[y, pl.ds(at0, n), cols[k]] = r * RD[y, :, cols[k]]
        blocks.append(to_block(target, at0, n, g, cols[k]))

    halos, blocks = [], []
    for k in range(nk + 1):
        if k < nk:
            for copy in parts[k]:
                copy.wait()
            scaled = []
            for y in range(ny):
                rd = inverse_diagonal(RHO, CX, cy, sz_ref, y, k)
                RD[y, :, cols[k]] = rd
                scaled.append(F[y, :, cols[k]] * rd)
            solved = smooth_z(scaled, LZ0[k], ny, n)
            for y in range(ny):
                UA[y + 1, own, cols[k]] = solved[y]
            if k == 0:
                enter()
            halos.append(halo(UA, ny, n, cols[k]))
        if k > 0:
            scaled_residual(UA, halos, W, blocks, k - 1)

    for copy in late:
        copy.wait()
    restrict_x = weights((n1, n + 2 * H), 1, H, 0, 0.375, 0.125)
    restrict_z = weights((B + 256, half), 0, 128, 0, 0.375, 0.125)
    CX1[...] = left_mul(mean_x, CX[...]) * 0.25
    for k in range(nk):
        fine_z = jnp.broadcast_to(sz_ref[:, cols[k]], (8, B))
        CZ1[:, k * half:k * half + half] = right_mul(fine_z, mean_z) * 0.25
        for y in range(ny1):
            pair = (RHO[2 * y, :, cols[k]] + RHO[2 * y + 1, :, cols[k]]) * 0.5
            RHO1[y, :, k * half:k * half + half] = right_mul(left_mul(mean_x, pair), mean_z)
    for y in range(ny1):
        for k in range(nk1):
            RD1[y, :, cols[k]] = inverse_diagonal(RHO1, CX1, cy1, CZ1, y, k)

    lx0 = split(LX0[...])
    halos, rims, sides, halos1 = [], [], [], []

    def fine_residual(k):
        arrive(halos[k])
        for y in range(ny):
            R0[y, own, cols[k]] = residual(F, UB, RHO, CX, cy, sz_ref, y, k)
        rims.append(halo_x(R0, (0, ny), n, cols[k]))

    def restrict_rows(k):
        arrive(rims[k])
        for y in range(ny):
            TX[y, :, cols[k]] = left_mul(restrict_x, R0[y, :, cols[k]])

    def restrict_columns(k):
        zs = slice(k * half, k * half + half)
        for y in range(ny):
            T1[y + 1, :, zs] = right_mul(window(TX, y, k, B, 128), restrict_z)
        sides.append(halo_y(T1, ny, slice(None), zs))

    def middle_rhs(k):
        arrive(sides[2 * k])
        arrive(sides[2 * k + 1])
        for y in range(ny1):
            a = 2 * y
            inner = T1[a + 1, :, cols[k]] + T1[a + 2, :, cols[k]]
            F1[y, :, cols[k]] = (T1[a, :, cols[k]] + 3.0 * inner + T1[a + 3, :, cols[k]]) * 0.125

    def middle_z(ref, before, rhs, k):
        scaled = [r * RD1[y, :, cols[k]] for y, r in enumerate(rhs)]
        solved = smooth_z(scaled, LZ1[k], ny1, n1)
        for y in range(ny1):
            u = solved[y] if before is None else before[y + 1, own1, cols[k]] + solved[y]
            ref[y + 1, own1, cols[k]] = u
        return halo(ref, ny1, n1, cols[k])

    def middle_first(k):
        middle_rhs(k)
        halos1.append(middle_z(M1, None, [F1[y, :, cols[k]] for y in range(ny1)], k))

    for k in range(nk):
        arrive(blocks[k])
        for y in range(ny):
            UB[y + 1, own, cols[k]] = UA[y + 1, own, cols[k]] + mm3(lx0, split(W[y, :, cols[k]]))
        halos.append(halo(UB, ny, n, cols[k]))
        if k >= 1:
            fine_residual(k - 1)
            restrict_rows(k - 1)
        if k >= 2:
            restrict_columns(k - 2)
    fine_residual(nk - 1)
    for k in range(nk1 - 1):
        middle_first(k)
    restrict_rows(nk - 1)
    restrict_columns(nk - 2)
    restrict_columns(nk - 1)
    middle_first(nk1 - 1)

    lx1 = split(LX1[...])

    def middle_x(ref, halos1, target, result, diagonals):
        sent = []
        for k in range(nk1):
            arrive(halos1[k])
            for y in range(ny1):
                r = residual(F1, ref, RHO1, CX1, cy1, CZ1, y, k)
                target[y, pl.ds(at1, n1), cols[k]] = r * RD1[y, :, cols[k]]
            sent.append(to_block(target, at1, n1, g1, cols[k]))
        edges = []
        for k in range(nk1):
            arrive(sent[k])
            for y in range(ny1):
                solved = mm3(lx1, split(target[y, :, cols[k]]))
                result[y + 1, own1, cols[k]] = ref[y + 1, own1, cols[k]] + solved
            edge = halo(result, ny1, n1, cols[k])
            if diagonals:
                edge = edge + halo_corners(result, ny1, n1, cols[k])
            edges.append(edge)
        return edges

    edges = middle_x(M1, halos1, V, M2, False)

    total = jnp.zeros((1, B), f32)
    for k in range(nk1):
        arrive(edges[k])
        for y in range(ny1):
            r = residual(F1, M2, RHO1, CX1, cy1, CZ1, y, k)
            total = total + jnp.sum(r, axis=0, keepdims=True)
    mean = jnp.sum(total, axis=1, keepdims=True) * (1.0 / (ny1 * n1 * nz1))
    lane = lax.broadcasted_iota(jnp.int32, CB.shape[1:], 1)
    G1[i] = jnp.where(lane == j * npx + i, mean, 0.0)
    arrive([push(G1.at[i], G1.at[i], lax.rem(i + s, npx), j) for s in range(1, npx)])
    G2[j] = jnp.sum(G1[...], axis=0)
    arrive([push(G2.at[j], G2.at[j], i, lax.rem(j + s, npy)) for s in range(1, npy)])
    means = jnp.sum(G2[...], axis=0)[0:1]
    arrive(neighbours)
    e = [jnp.sum(CB[s][0:1] * means, axis=1, keepdims=True) for s in range(5)]
    MP[1:ny1 + 1, own1, :] = M2[1:ny1 + 1, own1, :] + e[0]
    MP[1:ny1 + 1, 0:H, :] = M2[1:ny1 + 1, 0:H, :] + e[1]
    MP[1:ny1 + 1, n1 + H:n1 + 2 * H, :] = M2[1:ny1 + 1, n1 + H:n1 + 2 * H, :] + e[2]
    MP[0, own1, :] = M2[0, own1, :] + e[3]
    MP[ny1 + 1, own1, :] = M2[ny1 + 1, own1, :] + e[4]

    halos1 = []
    for k in range(nk1):
        rhs = [residual(F1, MP, RHO1, CX1, cy1, CZ1, y, k) for y in range(ny1)]
        halos1.append(middle_z(M3, MP, rhs, k))
    edges = middle_x(M3, halos1, V2, M4, True)

    raise_x = weights((n + 2 * H, n1 + 2 * H), 0, H, H, 0.75, 0.25)
    raise_z = weights((half + 256, B), 1, 0, 128, 0.75, 0.25)
    row = lax.broadcasted_iota(jnp.int32, (n + 2 * H, 1), 0)
    inside = jnp.logical_and(jnp.logical_or(row >= H, has_xm), jnp.logical_or(row < n + H, has_xp))
    arrived = []

    def prolong(k):
        while len(arrived) < min(k + 1, nk - 1) // 2 + 1:
            arrive(edges[len(arrived)])
            arrived.append(k)
        zs = cols[k]
        raised = [left_mul(raise_x, right_mul(window(M4, y, k, half, 128), raise_z)) for y in range(ny1 + 2)]
        for y in range(ny + 2):
            near = (y - 1) // 2 + 1
            other = near - 1 if (y - 1) % 2 == 0 else near + 1
            c = (3.0 * raised[near] + raised[other]) * 0.25
            if y == 0:
                UC[0, own, zs] = jnp.where(has_ym, UB[0, own, zs] + c[own], 0.0)
            elif y == ny + 1:
                UC[y, own, zs] = jnp.where(has_yp, UB[y, own, zs] + c[own], 0.0)
            else:
                UC[y, :, zs] = jnp.where(inside, UB[y, :, zs] + c, 0.0)

    halos, blocks = [], []
    prolong(0)
    for k in range(nk + 1):
        if k + 1 < nk:
            prolong(k + 1)
        if k < nk:
            scaled = [residual(F, UC, RHO, CX, cy, sz_ref, y, k) * RD[y, :, cols[k]] for y in range(ny)]
            solved = smooth_z(scaled, LZ0[k], ny, n)
            for y in range(ny):
                UD[y + 1, own, cols[k]] = UC[y + 1, own, cols[k]] + solved[y]
            halos.append(halo(UD, ny, n, cols[k]))
        if k > 0:
            scaled_residual(UD, halos, W2, blocks, k - 1)
    lx0 = split(LX0[...])
    stores = []
    for k in range(nk):
        arrive(blocks[k])
        for y in range(ny):
            OUT[y, :, cols[k]] = UD[y + 1, own, cols[k]] + mm3(lx0, split(W2[y, :, cols[k]]))
            store = pltpu.make_async_copy(OUT.at[y, :, cols[k]], out_ref.at[:, y, cols[k]], ls.at[len(stores)])
            store.start()
            stores.append(store)
    for sends, copy in pending:
        if sends is None:
            copy.wait_send()
        else:
            pl.when(sends)(copy.wait_send)
    for store in stores:
        store.wait()


def per_device(npx, npy, f, rho, sx, sy, sz, lz0, lx0, lz1, lx1, c):
    n, ny, nz = f.shape
    B = lz0.shape[-1]
    n1, ny1, nz1 = n // 2, ny // 2, nz // 2
    g, g1, nk = B // n, B // n1, nz // B
    lanes = -(-c.shape[1] // 128) * 128
    fine = pltpu.VMEM((ny, n, nz), f32)
    padded = pltpu.VMEM((ny + 2, n + 2 * H, nz), f32)
    coarse = pltpu.VMEM((ny1, n1, nz1), f32)
    coarse_padded = pltpu.VMEM((ny1 + 2, n1 + 2 * H, nz1), f32)
    copies = 4 + nk * (14 + 2 * g) + nk // 2 * (18 + 2 * g1) + npx + npy - 2
    anywhere = pl.BlockSpec(memory_space=pl.ANY)
    vmem = pl.BlockSpec(memory_space=pltpu.VMEM)
    smem = pl.BlockSpec(memory_space=pltpu.SMEM)
    return pl.pallas_call(
        functools.partial(kernel, (n, ny, nz, B, npx, npy)),
        out_shape=jax.ShapeDtypeStruct(f.shape, f32),
        in_specs=[anywhere, anywhere, vmem, smem, vmem, anywhere, anywhere, anywhere, anywhere, vmem],
        out_specs=anywhere,
        scratch_shapes=[
            fine, fine, fine, padded, padded, padded, padded,
            pltpu.VMEM((ny, B, nz), f32), pltpu.VMEM((ny, B, nz), f32),
            pltpu.VMEM((ny, n + 2 * H, nz), f32), pltpu.VMEM((ny, n1, nz), f32), pltpu.VMEM((ny + 2, n1, nz1), f32),
            coarse, coarse, coarse,
            coarse_padded, coarse_padded, coarse_padded, coarse_padded, coarse_padded,
            pltpu.VMEM((ny1, B, nz1), f32), pltpu.VMEM((ny1, B, nz1), f32),
            pltpu.VMEM((npx, 8, lanes), f32), pltpu.VMEM((npy, 8, lanes), f32), pltpu.VMEM((5, 8, lanes), f32),
            pltpu.VMEM((n, B), f32), pltpu.VMEM((n1, B), f32), pltpu.VMEM((8, nz1), f32),
            pltpu.VMEM(lz0.shape, f32), pltpu.VMEM(lz1.shape, f32),
            pltpu.VMEM((n, B), f32), pltpu.VMEM((n1, B), f32), fine,
            pltpu.SemaphoreType.DMA((copies,)), pltpu.SemaphoreType.DMA((copies,)),
            pltpu.SemaphoreType.DMA((nk * (2 * ny + 1) + 3,)),
        ],
        compiler_params=pltpu.CompilerParams(
            collective_id=0, has_side_effects=True, vmem_limit_bytes=56 * 1024 * 1024
        ),
    )(f, rho, sx.reshape(1, n), sy, sz.reshape(1, nz), lz0, lx0, lz1, lx1, c)


def solution(mesh):
    placed = (
        P("px", "py", None), P("px", "py", None), P("px"), P("py"),
        P(), P(), P(), P(), P(), P(("py", "px"), None),
    )
    body = functools.partial(per_device, mesh.shape["px"], mesh.shape["py"])
    return jax.shard_map(
        body, mesh=mesh, in_specs=placed, out_specs=P("px", "py", None), check_vma=False
    )
```

```python
import functools

import jax
import jax.numpy as jnp
from jax import lax
from jax.experimental import pallas as pl
from jax.experimental.pallas import tpu as pltpu
from jax.sharding import PartitionSpec as P

f32 = jnp.float32
bf16 = jnp.bfloat16
MESH = pl.DeviceIdType.MESH
shift_term = 0.1
H = 8


def split(a):
    hi = a.astype(bf16)
    return hi, (a - hi.astype(f32)).astype(bf16)


def mm(a, b, transposed=False):
    dims = (((1,), (1 if transposed else 0,)), ((), ()))
    return lax.dot_general(a, b, dims, preferred_element_type=f32)


def mm3(a, b, transposed=False):
    (ah, al), (bh, bl) = a, b
    axis = 1 if transposed else 0
    return mm(
        jnp.concatenate([ah, ah, al], axis=1), jnp.concatenate([bh, bl, bh], axis=axis), transposed
    )


def strips(rows, body):
    step = min(rows, 32)

    def at(t, carry):
        body(pl.multiple_of(t * step, step), step)
        return carry

    lax.fori_loop(0, rows // step, at, 0)


def weights(shape, fine_dim, fine_pad, coarse_pad, inner, outer):
    fine = lax.broadcasted_iota(jnp.int32, shape, fine_dim) - fine_pad
    coarse = lax.broadcasted_iota(jnp.int32, shape, 1 - fine_dim) - coarse_pad
    d = fine - 2 * coarse
    near = jnp.where((d == 0) | (d == 1), inner, 0.0)
    if outer:
        near = jnp.where((d == -1) | (d == 2), outer, near)
    return near.astype(bf16)


def left_mul(m, v):
    hi, lo = split(v)
    return mm(m, hi) + mm(m, lo)


def right_mul(v, m):
    rows = v.shape[0]
    both = mm(jnp.concatenate(split(v), axis=0), m)
    return both[:rows] + both[rows:]


def kernel(
    dims,
    f_in, rho_in, sx_ref, sy_ref, sz_ref, lz0_in, lx0_in, lz1_in, lx1_in, c_ref,
    out_ref,
    F, RHO, RD, UA, UB, UC, UD, W, W2, R0, TX, T1, F1, RHO1, RD1,
    M1, M2, MP, M3, M4, V, V2, G1, G2, CB, CX, CX1, CZ1, LZ0, LZ1, LX0, LX1, SH, SL, OUT,
    ss, rs, ls,
):
    n, ny, nz, B, npx, npy = dims
    n1, ny1, nz1 = n // 2, ny // 2, nz // 2
    nk, nk1 = nz // B, nz1 // B
    g, g1 = B // n, B // n1
    i, j = lax.axis_index("px"), lax.axis_index("py")
    has_xm, has_xp = i > 0, i < npx - 1
    has_ym, has_yp = j > 0, j < npy - 1
    xm, xp = lax.rem(i + npx - 1, npx), lax.rem(i + 1, npx)
    ym, yp = lax.rem(j + npy - 1, npy), lax.rem(j + 1, npy)

    loads = []

    def load(src, dst):
        copy = pltpu.make_async_copy(src, dst, ls.at[len(loads)])
        copy.start()
        loads.append(copy)
        return copy

    half = B // 2
    cols = [slice(k * B, k * B + B) for k in range(nk)]
    parts = []
    for k in range(nk):
        part = [load(lz0_in.at[k], LZ0.at[k])]
        for y in range(ny):
            part.append(load(f_in.at[:, y, cols[k]], F.at[y, :, cols[k]]))
            part.append(load(rho_in.at[:, y, cols[k]], RHO.at[y, :, cols[k]]))
        parts.append(part)
    at0 = pl.multiple_of(lax.rem(i, g) * n, n)
    at1 = pl.multiple_of(lax.rem(i, g1) * n1, n1)
    late = [
        load(lx0_in.at[i // g, pl.ds(at0, n), :], LX0),
        load(lx1_in.at[i // g1, pl.ds(at1, n1), :], LX1),
        load(lz1_in, LZ1),
    ]

    for ref in (UA, UB, UD, R0, M1, M2, M3, M4):
        rows = ref.shape[1]

        @pl.when(jnp.logical_not(has_xm))
        def _(ref=ref):
            ref[:, 0:H, :] = jnp.zeros((ref.shape[0], H, ref.shape[2]), f32)

        @pl.when(jnp.logical_not(has_xp))
        def _(ref=ref, rows=rows):
            ref[:, rows - H:rows, :] = jnp.zeros((ref.shape[0], H, ref.shape[2]), f32)

    for ref in (UA, UB, UD, T1, M1, M2, M3, M4):
        planes = ref.shape[0]

        @pl.when(jnp.logical_not(has_ym))
        def _(ref=ref):
            ref[0] = jnp.zeros(ref.shape[1:], f32)

        @pl.when(jnp.logical_not(has_yp))
        def _(ref=ref, planes=planes):
            ref[planes - 1] = jnp.zeros(ref.shape[1:], f32)

    count = c_ref.shape[1]
    CB[...] = jnp.zeros(CB.shape, f32)
    CB[0, :, 0:count] = jnp.broadcast_to(c_ref[...], (8, count))

    barrier = pltpu.get_barrier_semaphore()
    for s in range(1, npx):
        pl.semaphore_signal(barrier, inc=1, device_id={"px": lax.rem(i + s, npx), "py": j}, device_id_type=MESH)
    for s in range(1, npy):
        pl.semaphore_signal(barrier, inc=1, device_id={"px": i, "py": lax.rem(j + s, npy)}, device_id_type=MESH)
    for to_x in (xm, xp):
        for to_y in (ym, yp):
            pl.semaphore_signal(barrier, inc=1, device_id={"px": to_x, "py": to_y}, device_id_type=MESH)

    pending = []

    def push(src, dst, to_x, to_y, sends=None, receives=None):
        at = len(pending)
        copy = pltpu.make_async_remote_copy(
            src_ref=src, dst_ref=dst, send_sem=ss.at[at], recv_sem=rs.at[at],
            device_id={"px": to_x, "py": to_y}, device_id_type=MESH,
        )
        if sends is None:
            copy.start()
        else:
            pl.when(sends)(copy.start)
        pending.append((sends, copy))
        return receives, copy

    def arrive(handles):
        for receives, copy in handles:
            if receives is None:
                copy.wait_recv()
            else:
                pl.when(receives)(copy.wait_recv)

    def halo_x(ref, planes, rows, zs):
        a, b = planes
        return [
            push(ref.at[a:b, rows:rows + H, zs], ref.at[a:b, 0:H, zs], xp, j, has_xp, has_xm),
            push(ref.at[a:b, H:2 * H, zs], ref.at[a:b, rows + H:rows + 2 * H, zs], xm, j, has_xm, has_xp),
        ]

    def halo_y(ref, planes, r, zs):
        return [
            push(ref.at[planes, r, zs], ref.at[0, r, zs], i, yp, has_yp, has_ym),
            push(ref.at[1, r, zs], ref.at[planes + 1, r, zs], i, ym, has_ym, has_yp),
        ]

    def halo(ref, planes, rows, zs):
        return halo_y(ref, planes, slice(H, H + rows), zs) + halo_x(ref, (1, planes + 1), rows, zs)

    def halo_corners(ref, planes, rows, zs):
        both = jnp.logical_and
        low, high = slice(0, H), slice(rows + H, rows + 2 * H)
        first, last = slice(H, 2 * H), slice(rows, rows + H)
        return [
            push(ref.at[planes, last, zs], ref.at[0, low, zs], xp, yp, both(has_xp, has_yp), both(has_xm, has_ym)),
            push(ref.at[1, last, zs], ref.at[planes + 1, low, zs], xp, ym, both(has_xp, has_ym), both(has_xm, has_yp)),
            push(ref.at[planes, first, zs], ref.at[0, high, zs], xm, yp, both(has_xm, has_yp), both(has_xp, has_ym)),
            push(ref.at[1, first, zs], ref.at[planes + 1, high, zs], xm, ym, both(has_xm, has_ym), both(has_xp, has_yp)),
        ]

    def to_block(ref, at, rows, peers, zs):
        here = lax.rem(i, peers)
        base = i - here
        mine = ref.at[:, pl.ds(at, rows), zs]
        return [push(mine, mine, base + lax.rem(here + s, peers), j) for s in range(1, peers)]

    def residual(rhs, ref, rho, cx, cys, cz, y, k, r, step):
        lo = k * B
        zs = slice(lo, lo + B)
        here = pl.ds(r, step)
        own = pl.ds(pl.multiple_of(r + H, H), step)
        block = ref[y + 1, pl.ds(r, step + 2 * H), zs]
        c = block[H:H + step]
        near_x = block[H - 1:H - 1 + step] + block[H + 1:H + 1 + step]
        near_y = ref[y, own, zs] + ref[y + 2, own, zs]
        blank = jnp.zeros((step, 128), f32)
        left = ref[y + 1, own, lo - 128:lo] if lo > 0 else blank
        right = ref[y + 1, own, lo + B:lo + B + 128] if lo + B < ref.shape[2] else blank
        wide = jnp.concatenate([left, c, right], axis=1)
        near_z = (pltpu.roll(wide, 1, 1) + pltpu.roll(wide, B + 255, 1))[:, 128:128 + B]
        twice = 2.0 * c
        stencil = (
            cx[here, :] * (twice - near_x) + cys[y] * (twice - near_y) + cz[0:1, zs] * (twice - near_z)
        )
        return rhs[y, here, zs] - (shift_term * c + rho[y, here, zs] * stencil)

    def inverse_diagonal(rho, cx, cys, cz, y, k, r, step):
        zs = slice(k * B, k * B + B)
        here = pl.ds(r, step)
        return 1.0 / (shift_term + 2.0 * rho[y, here, zs] * (cx[here, :] + cys[y] + cz[0:1, zs]))

    square = (n, n)
    diag = lax.broadcasted_iota(jnp.int32, square, 0) == lax.broadcasted_iota(jnp.int32, square, 1)
    column = jnp.sum(jnp.where(diag, jnp.broadcast_to(sx_ref[...], square), 0.0), axis=1, keepdims=True)
    CX[...] = jnp.broadcast_to(column, (n, B))
    cy = [sy_ref[y] for y in range(ny)]
    cy1 = [(cy[2 * y] + cy[2 * y + 1]) * 0.125 for y in range(ny1)]

    neighbours = []

    def enter():
        pl.semaphore_wait(barrier, npx + npy + 2)
        neighbours.extend([
            push(CB.at[0], CB.at[1], xp, j, has_xp, has_xm),
            push(CB.at[0], CB.at[2], xm, j, has_xm, has_xp),
            push(CB.at[0], CB.at[3], i, yp, has_yp, has_ym),
            push(CB.at[0], CB.at[4], i, ym, has_ym, has_yp),
        ])

    def keep(value, y, rows, r, step):
        at = pl.ds(pl.multiple_of(y * rows + r, step), step)
        SH[at, :], SL[at, :] = split(value)

    def smooth_z(block, planes, rows):
        z = mm3((SH[0:planes * rows], SL[0:planes * rows]), split(block), True)
        return [z[y * rows:(y + 1) * rows] for y in range(planes)]

    def window(ref, y, k, width, side):
        lo = k * width
        parts = [ref[y, :, lo:lo + width]]
        blank = jnp.zeros((ref.shape[1], side), f32)
        parts.insert(0, ref[y, :, lo - side:lo] if lo > 0 else blank)
        parts.append(ref[y, :, lo + width:lo + width + side] if lo + width < ref.shape[2] else blank)
        return jnp.concatenate(parts, axis=1)

    own = slice(H, H + n)
    own1 = slice(H, H + n1)
    mean_x = weights((n1, n), 1, 0, 0, 0.5, 0.0)
    mean_z = weights((B, half), 0, 0, 0, 0.5, 0.0)

    def scaled_residual(ref, halos, target, blocks, k):
        arrive(halos[k])

        def body(r, step):
            for y in range(ny):
                v = residual(F, ref, RHO, CX, cy, sz_ref, y, k, r, step)
                target[y, pl.ds(pl.multiple_of(at0 + r, step), step), cols[k]] = v * RD[y, pl.ds(r, step), cols[k]]

        strips(n, body)
        blocks.append(to_block(target, at0, n, g, cols[k]))

    halos, blocks = [], []
    for k in range(nk + 1):
        if k < nk:
            for copy in parts[k]:
                copy.wait()

            def body(r, step, k=k):
                here = pl.ds(r, step)
                for y in range(ny):
                    rd = inverse_diagonal(RHO, CX, cy, sz_ref, y, k, r, step)
                    RD[y, here, cols[k]] = rd
                    keep(F[y, here, cols[k]] * rd, y, n, r, step)

            strips(n, body)
            solved = smooth_z(LZ0[k], ny, n)
            for y in range(ny):
                UA[y + 1, own, cols[k]] = solved[y]
            if k == 0:
                enter()
            halos.append(halo(UA, ny, n, cols[k]))
        if k > 0:
            scaled_residual(UA, halos, W, blocks, k - 1)

    for copy in late:
        copy.wait()
    restrict_x = weights((n1, n + 2 * H), 1, H, 0, 0.375, 0.125)
    restrict_z = weights((B + 256, half), 0, 128, 0, 0.375, 0.125)
    CX1[...] = left_mul(mean_x, CX[...]) * 0.25
    for k in range(nk):
        fine_z = jnp.broadcast_to(sz_ref[:, cols[k]], (8, B))
        CZ1[:, k * half:k * half + half] = right_mul(fine_z, mean_z) * 0.25
        for y in range(ny1):
            pair = (RHO[2 * y, :, cols[k]] + RHO[2 * y + 1, :, cols[k]]) * 0.5
            RHO1[y, :, k * half:k * half + half] = right_mul(left_mul(mean_x, pair), mean_z)
    for y in range(ny1):
        for k in range(nk1):

            def body(r, step, y=y, k=k):
                RD1[y, pl.ds(r, step), cols[k]] = inverse_diagonal(RHO1, CX1, cy1, CZ1, y, k, r, step)

            strips(n1, body)

    lx0 = split(LX0[...])
    halos, rims, sides, halos1 = [], [], [], []

    def fine_residual(k):
        arrive(halos[k])

        def body(r, step):
            for y in range(ny):
                v = residual(F, UB, RHO, CX, cy, sz_ref, y, k, r, step)
                R0[y, pl.ds(pl.multiple_of(r + H, H), step), cols[k]] = v

        strips(n, body)
        rims.append(halo_x(R0, (0, ny), n, cols[k]))

    def restrict_rows(k):
        arrive(rims[k])
        for y in range(ny):
            TX[y, :, cols[k]] = left_mul(restrict_x, R0[y, :, cols[k]])

    def restrict_columns(k):
        zs = slice(k * half, k * half + half)
        for y in range(ny):
            T1[y + 1, :, zs] = right_mul(window(TX, y, k, B, 128), restrict_z)
        sides.append(halo_y(T1, ny, slice(None), zs))

    def middle_rhs(k):
        arrive(sides[2 * k])
        arrive(sides[2 * k + 1])
        for y in range(ny1):
            a = 2 * y
            inner = T1[a + 1, :, cols[k]] + T1[a + 2, :, cols[k]]
            F1[y, :, cols[k]] = (T1[a, :, cols[k]] + 3.0 * inner + T1[a + 3, :, cols[k]]) * 0.125

    def middle_z(ref, before, rhs, k):

        def body(r, step):
            for y in range(ny1):
                keep(rhs(y, r, step) * RD1[y, pl.ds(r, step), cols[k]], y, n1, r, step)

        strips(n1, body)
        solved = smooth_z(LZ1[k], ny1, n1)
        for y in range(ny1):
            u = solved[y] if before is None else before[y + 1, own1, cols[k]] + solved[y]
            ref[y + 1, own1, cols[k]] = u
        return halo(ref, ny1, n1, cols[k])

    def middle_first(k):
        middle_rhs(k)
        halos1.append(middle_z(M1, None, lambda y, r, step: F1[y, pl.ds(r, step), cols[k]], k))

    for k in range(nk):
        arrive(blocks[k])
        for y in range(ny):
            UB[y + 1, own, cols[k]] = UA[y + 1, own, cols[k]] + mm3(lx0, split(W[y, :, cols[k]]))
        halos.append(halo(UB, ny, n, cols[k]))
        if k >= 1:
            fine_residual(k - 1)
            restrict_rows(k - 1)
        if k >= 2:
            restrict_columns(k - 2)
    fine_residual(nk - 1)
    for k in range(nk1 - 1):
        middle_first(k)
    restrict_rows(nk - 1)
    restrict_columns(nk - 2)
    restrict_columns(nk - 1)
    middle_first(nk1 - 1)

    lx1 = split(LX1[...])

    def middle_x(ref, halos1, target, result, diagonals):
        sent = []
        for k in range(nk1):
            arrive(halos1[k])

            def body(r, step, k=k):
                for y in range(ny1):
                    v = residual(F1, ref, RHO1, CX1, cy1, CZ1, y, k, r, step)
                    at = pl.ds(pl.multiple_of(at1 + r, step), step)
                    target[y, at, cols[k]] = v * RD1[y, pl.ds(r, step), cols[k]]

            strips(n1, body)
            sent.append(to_block(target, at1, n1, g1, cols[k]))
        edges = []
        for k in range(nk1):
            arrive(sent[k])
            for y in range(ny1):
                solved = mm3(lx1, split(target[y, :, cols[k]]))
                result[y + 1, own1, cols[k]] = ref[y + 1, own1, cols[k]] + solved
            edge = halo(result, ny1, n1, cols[k])
            if diagonals:
                edge = edge + halo_corners(result, ny1, n1, cols[k])
            edges.append(edge)
        return edges

    edges = middle_x(M1, halos1, V, M2, False)

    total = jnp.zeros((1, B), f32)
    for k in range(nk1):
        arrive(edges[k])
        step1 = min(n1, 32)

        def add(t, total, k=k, step1=step1):
            r = pl.multiple_of(t * step1, step1)
            for y in range(ny1):
                v = residual(F1, M2, RHO1, CX1, cy1, CZ1, y, k, r, step1)
                total = total + jnp.sum(v, axis=0, keepdims=True)
            return total

        total = lax.fori_loop(0, n1 // step1, add, total)
    mean = jnp.sum(total, axis=1, keepdims=True) * (1.0 / (ny1 * n1 * nz1))
    lane = lax.broadcasted_iota(jnp.int32, CB.shape[1:], 1)
    G1[i] = jnp.where(lane == j * npx + i, mean, 0.0)
    arrive([push(G1.at[i], G1.at[i], lax.rem(i + s, npx), j) for s in range(1, npx)])
    G2[j] = jnp.sum(G1[...], axis=0)
    arrive([push(G2.at[j], G2.at[j], i, lax.rem(j + s, npy)) for s in range(1, npy)])
    means = jnp.sum(G2[...], axis=0)[0:1]
    arrive(neighbours)
    e = [jnp.sum(CB[s][0:1] * means, axis=1, keepdims=True) for s in range(5)]
    MP[1:ny1 + 1, own1, :] = M2[1:ny1 + 1, own1, :] + e[0]
    MP[1:ny1 + 1, 0:H, :] = M2[1:ny1 + 1, 0:H, :] + e[1]
    MP[1:ny1 + 1, n1 + H:n1 + 2 * H, :] = M2[1:ny1 + 1, n1 + H:n1 + 2 * H, :] + e[2]
    MP[0, own1, :] = M2[0, own1, :] + e[3]
    MP[ny1 + 1, own1, :] = M2[ny1 + 1, own1, :] + e[4]

    halos1 = []
    for k in range(nk1):

        def rhs(y, r, step, k=k):
            return residual(F1, MP, RHO1, CX1, cy1, CZ1, y, k, r, step)

        halos1.append(middle_z(M3, MP, rhs, k))
    edges = middle_x(M3, halos1, V2, M4, True)

    raise_x = weights((n + 2 * H, n1 + 2 * H), 0, H, H, 0.75, 0.25)
    raise_z = weights((half + 256, B), 1, 0, 128, 0.75, 0.25)
    row = lax.broadcasted_iota(jnp.int32, (n + 2 * H, 1), 0)
    inside = jnp.logical_and(jnp.logical_or(row >= H, has_xm), jnp.logical_or(row < n + H, has_xp))
    arrived = []

    def prolong(k):
        while len(arrived) < min(k + 1, nk - 1) // 2 + 1:
            arrive(edges[len(arrived)])
            arrived.append(k)
        zs = cols[k]
        rows = n1 + 2 * H
        wide = right_mul(jnp.concatenate([window(M4, y, k, half, 128) for y in range(ny1 + 2)], axis=0), raise_z)
        raised = [left_mul(raise_x, wide[y * rows:(y + 1) * rows]) for y in range(ny1 + 2)]
        for y in range(ny + 2):
            near = (y - 1) // 2 + 1
            other = near - 1 if (y - 1) % 2 == 0 else near + 1
            c = (3.0 * raised[near] + raised[other]) * 0.25
            if y == 0:
                UC[0, own, zs] = jnp.where(has_ym, UB[0, own, zs] + c[own], 0.0)
            elif y == ny + 1:
                UC[y, own, zs] = jnp.where(has_yp, UB[y, own, zs] + c[own], 0.0)
            else:
                UC[y, :, zs] = jnp.where(inside, UB[y, :, zs] + c, 0.0)

    halos, blocks = [], []
    prolong(0)
    for k in range(nk + 1):
        if k + 1 < nk:
            prolong(k + 1)
        if k < nk:

            def body(r, step, k=k):
                for y in range(ny):
                    v = residual(F, UC, RHO, CX, cy, sz_ref, y, k, r, step)
                    keep(v * RD[y, pl.ds(r, step), cols[k]], y, n, r, step)

            strips(n, body)
            solved = smooth_z(LZ0[k], ny, n)
            for y in range(ny):
                UD[y + 1, own, cols[k]] = UC[y + 1, own, cols[k]] + solved[y]
            halos.append(halo(UD, ny, n, cols[k]))
        if k > 0:
            scaled_residual(UD, halos, W2, blocks, k - 1)
    lx0 = split(LX0[...])
    stores = []
    for k in range(nk):
        arrive(blocks[k])
        for y in range(ny):
            OUT[y, :, cols[k]] = UD[y + 1, own, cols[k]] + mm3(lx0, split(W2[y, :, cols[k]]))
            store = pltpu.make_async_copy(OUT.at[y, :, cols[k]], out_ref.at[:, y, cols[k]], ls.at[len(stores)])
            store.start()
            stores.append(store)
    for sends, copy in pending:
        if sends is None:
            copy.wait_send()
        else:
            pl.when(sends)(copy.wait_send)
    for store in stores:
        store.wait()


def per_device(npx, npy, f, rho, sx, sy, sz, lz0, lx0, lz1, lx1, c):
    n, ny, nz = f.shape
    B = lz0.shape[-1]
    n1, ny1, nz1 = n // 2, ny // 2, nz // 2
    g, g1, nk = B // n, B // n1, nz // B
    lanes = -(-c.shape[1] // 128) * 128
    fine = pltpu.VMEM((ny, n, nz), f32)
    padded = pltpu.VMEM((ny + 2, n + 2 * H, nz), f32)
    coarse = pltpu.VMEM((ny1, n1, nz1), f32)
    coarse_padded = pltpu.VMEM((ny1 + 2, n1 + 2 * H, nz1), f32)
    copies = 4 + nk * (14 + 2 * g) + nk // 2 * (18 + 2 * g1) + npx + npy - 2
    anywhere = pl.BlockSpec(memory_space=pl.ANY)
    vmem = pl.BlockSpec(memory_space=pltpu.VMEM)
    smem = pl.BlockSpec(memory_space=pltpu.SMEM)
    return pl.pallas_call(
        functools.partial(kernel, (n, ny, nz, B, npx, npy)),
        out_shape=jax.ShapeDtypeStruct(f.shape, f32),
        in_specs=[anywhere, anywhere, vmem, smem, vmem, anywhere, anywhere, anywhere, anywhere, vmem],
        out_specs=anywhere,
        scratch_shapes=[
            fine, fine, fine, padded, padded, padded, padded,
            pltpu.VMEM((ny, B, nz), f32), pltpu.VMEM((ny, B, nz), f32),
            pltpu.VMEM((ny, n + 2 * H, nz), f32), pltpu.VMEM((ny, n1, nz), f32), pltpu.VMEM((ny + 2, n1, nz1), f32),
            coarse, coarse, coarse,
            coarse_padded, coarse_padded, coarse_padded, coarse_padded, coarse_padded,
            pltpu.VMEM((ny1, B, nz1), f32), pltpu.VMEM((ny1, B, nz1), f32),
            pltpu.VMEM((npx, 8, lanes), f32), pltpu.VMEM((npy, 8, lanes), f32), pltpu.VMEM((5, 8, lanes), f32),
            pltpu.VMEM((n, B), f32), pltpu.VMEM((n1, B), f32), pltpu.VMEM((8, nz1), f32),
            pltpu.VMEM(lz0.shape, f32), pltpu.VMEM(lz1.shape, f32),
            pltpu.VMEM((n, B), f32), pltpu.VMEM((n1, B), f32),
            pltpu.VMEM((ny * n, B), bf16), pltpu.VMEM((ny * n, B), bf16), fine,
            pltpu.SemaphoreType.DMA((copies,)), pltpu.SemaphoreType.DMA((copies,)),
            pltpu.SemaphoreType.DMA((nk * (2 * ny + 1) + 3,)),
        ],
        compiler_params=pltpu.CompilerParams(
            collective_id=0, has_side_effects=True, vmem_limit_bytes=56 * 1024 * 1024
        ),
    )(f, rho, sx.reshape(1, n), sy, sz.reshape(1, nz), lz0, lx0, lz1, lx1, c)


def solution(mesh):
    placed = (
        P("px", "py", None), P("px", "py", None), P("px"), P("py"),
        P(), P(), P(), P(), P(), P(("py", "px"), None),
    )
    body = functools.partial(per_device, mesh.shape["px"], mesh.shape["py"])
    return jax.shard_map(
        body, mesh=mesh, in_specs=placed, out_specs=P("px", "py", None), check_vma=False
    )
```

```python
import functools

import jax
import jax.numpy as jnp
from jax import lax
from jax.experimental import pallas as pl
from jax.experimental.pallas import tpu as pltpu
from jax.sharding import PartitionSpec as P

f32 = jnp.float32
bf16 = jnp.bfloat16
MESH = pl.DeviceIdType.MESH
shift_term = 0.1
H = 8


def split(a):
    hi = a.astype(bf16)
    return hi, (a - hi.astype(f32)).astype(bf16)


def mm(a, b, transposed=False):
    dims = (((1,), (1 if transposed else 0,)), ((), ()))
    return lax.dot_general(a, b, dims, preferred_element_type=f32)


def mm3(a, b, transposed=False):
    (ah, al), (bh, bl) = a, b
    axis = 1 if transposed else 0
    return mm(
        jnp.concatenate([ah, ah, al], axis=1), jnp.concatenate([bh, bl, bh], axis=axis), transposed
    )


def strips(rows, body):
    step = min(rows, 32)

    def at(t, carry):
        body(pl.multiple_of(t * step, step), step)
        return carry

    lax.fori_loop(0, rows // step, at, 0)


def weights(shape, fine_dim, fine_pad, coarse_pad, inner, outer):
    fine = lax.broadcasted_iota(jnp.int32, shape, fine_dim) - fine_pad
    coarse = lax.broadcasted_iota(jnp.int32, shape, 1 - fine_dim) - coarse_pad
    d = fine - 2 * coarse
    near = jnp.where((d == 0) | (d == 1), inner, 0.0)
    if outer:
        near = jnp.where((d == -1) | (d == 2), outer, near)
    return near.astype(bf16)


def left_mul(m, v):
    hi, lo = split(v)
    return mm(m, hi) + mm(m, lo)


def right_mul(v, m):
    rows = v.shape[0]
    both = mm(jnp.concatenate(split(v), axis=0), m)
    return both[:rows] + both[rows:]


def kernel(
    dims,
    f_in, rho_in, sx_ref, sy_ref, sz_ref, lz0_in, lx0_in, lz1_in, lx1_in, c_ref,
    out_ref,
    F, RHO, RD, UA, UB, UC, UD, W, W2, R0, TX, T1, F1, RHO1, RD1,
    M1, M2, MP, M3, M4, V, V2, G1, G2, CB, CX, CX1, CZ1, LZ0, LZ1, LX0, LX1, SH, SL, OUT,
    ss, rs, ls,
):
    n, ny, nz, B, npx, npy = dims
    n1, ny1, nz1 = n // 2, ny // 2, nz // 2
    nk, nk1 = nz // B, nz1 // B
    g, g1 = B // n, B // n1
    i, j = lax.axis_index("px"), lax.axis_index("py")
    has_xm, has_xp = i > 0, i < npx - 1
    has_ym, has_yp = j > 0, j < npy - 1
    xm, xp = lax.rem(i + npx - 1, npx), lax.rem(i + 1, npx)
    ym, yp = lax.rem(j + npy - 1, npy), lax.rem(j + 1, npy)

    loads = []

    def load(src, dst):
        copy = pltpu.make_async_copy(src, dst, ls.at[len(loads)])
        copy.start()
        loads.append(copy)
        return copy

    half = B // 2
    cols = [slice(k * B, k * B + B) for k in range(nk)]
    parts = []
    for k in range(nk):
        part = [load(lz0_in.at[k], LZ0.at[k])]
        for y in range(ny):
            part.append(load(f_in.at[:, y, cols[k]], F.at[y, :, cols[k]]))
            part.append(load(rho_in.at[:, y, cols[k]], RHO.at[y, :, cols[k]]))
        parts.append(part)
    at0 = pl.multiple_of(lax.rem(i, g) * n, n)
    at1 = pl.multiple_of(lax.rem(i, g1) * n1, n1)
    late = [
        load(lx0_in.at[i // g, pl.ds(at0, n), :], LX0),
        load(lx1_in.at[i // g1, pl.ds(at1, n1), :], LX1),
        load(lz1_in, LZ1),
    ]

    for ref in (UA, UB, UD, R0, M1, M2, M3, M4):
        rows = ref.shape[1]

        @pl.when(jnp.logical_not(has_xm))
        def _(ref=ref):
            ref[:, 0:H, :] = jnp.zeros((ref.shape[0], H, ref.shape[2]), f32)

        @pl.when(jnp.logical_not(has_xp))
        def _(ref=ref, rows=rows):
            ref[:, rows - H:rows, :] = jnp.zeros((ref.shape[0], H, ref.shape[2]), f32)

    for ref in (UA, UB, UD, T1, M1, M2, M3, M4):
        planes = ref.shape[0]

        @pl.when(jnp.logical_not(has_ym))
        def _(ref=ref):
            ref[0] = jnp.zeros(ref.shape[1:], f32)

        @pl.when(jnp.logical_not(has_yp))
        def _(ref=ref, planes=planes):
            ref[planes - 1] = jnp.zeros(ref.shape[1:], f32)

    count = c_ref.shape[1]
    CB[...] = jnp.zeros(CB.shape, f32)
    CB[0, :, 0:count] = jnp.broadcast_to(c_ref[...], (8, count))

    barrier = pltpu.get_barrier_semaphore()
    for s in range(1, npx):
        pl.semaphore_signal(barrier, inc=1, device_id={"px": lax.rem(i + s, npx), "py": j}, device_id_type=MESH)
    for s in range(1, npy):
        pl.semaphore_signal(barrier, inc=1, device_id={"px": i, "py": lax.rem(j + s, npy)}, device_id_type=MESH)
    for to_x in (xm, xp):
        for to_y in (ym, yp):
            pl.semaphore_signal(barrier, inc=1, device_id={"px": to_x, "py": to_y}, device_id_type=MESH)

    pending = []

    def push(src, dst, to_x, to_y, sends=None, receives=None):
        at = len(pending)
        copy = pltpu.make_async_remote_copy(
            src_ref=src, dst_ref=dst, send_sem=ss.at[at], recv_sem=rs.at[at],
            device_id={"px": to_x, "py": to_y}, device_id_type=MESH,
        )
        if sends is None:
            copy.start()
        else:
            pl.when(sends)(copy.start)
        pending.append((sends, copy))
        return receives, copy

    def arrive(handles):
        while handles:
            receives, copy = handles.pop(0)
            if receives is None:
                copy.wait_recv()
            else:
                pl.when(receives)(copy.wait_recv)

    drained = []

    def drain(until):
        for sends, copy in pending[len(drained):until]:
            drained.append(copy)
            if sends is None:
                copy.wait_send()
            else:
                pl.when(sends)(copy.wait_send)

    def grouped(groups, width, k, handles, start):
        for a, b in groups:
            if k == b - 1:
                handles.extend([start(slice(a * width, b * width))] * (b - a))

    def halo_x(ref, planes, rows, zs):
        a, b = planes
        return [
            push(ref.at[a:b, rows:rows + H, zs], ref.at[a:b, 0:H, zs], xp, j, has_xp, has_xm),
            push(ref.at[a:b, H:2 * H, zs], ref.at[a:b, rows + H:rows + 2 * H, zs], xm, j, has_xm, has_xp),
        ]

    def halo_y(ref, planes, r, zs):
        return [
            push(ref.at[planes, r, zs], ref.at[0, r, zs], i, yp, has_yp, has_ym),
            push(ref.at[1, r, zs], ref.at[planes + 1, r, zs], i, ym, has_ym, has_yp),
        ]

    def halo(ref, planes, rows, zs):
        return halo_y(ref, planes, slice(H, H + rows), zs) + halo_x(ref, (1, planes + 1), rows, zs)

    def halo_corners(ref, planes, rows, zs):
        both = jnp.logical_and
        low, high = slice(0, H), slice(rows + H, rows + 2 * H)
        first, last = slice(H, 2 * H), slice(rows, rows + H)
        return [
            push(ref.at[planes, last, zs], ref.at[0, low, zs], xp, yp, both(has_xp, has_yp), both(has_xm, has_ym)),
            push(ref.at[1, last, zs], ref.at[planes + 1, low, zs], xp, ym, both(has_xp, has_ym), both(has_xm, has_yp)),
            push(ref.at[planes, first, zs], ref.at[0, high, zs], xm, yp, both(has_xm, has_yp), both(has_xp, has_ym)),
            push(ref.at[1, first, zs], ref.at[planes + 1, high, zs], xm, ym, both(has_xm, has_ym), both(has_xp, has_yp)),
        ]

    def to_block(ref, at, rows, peers, zs):
        here = lax.rem(i, peers)
        base = i - here
        mine = ref.at[:, pl.ds(at, rows), zs]
        return [push(mine, mine, base + lax.rem(here + s, peers), j) for s in range(1, peers)]

    def residual(rhs, ref, rho, cx, cys, cz, y, k, r, step):
        lo = k * B
        zs = slice(lo, lo + B)
        here = pl.ds(r, step)
        own = pl.ds(pl.multiple_of(r + H, H), step)
        block = ref[y + 1, pl.ds(r, step + 2 * H), zs]
        c = block[H:H + step]
        near_x = block[H - 1:H - 1 + step] + block[H + 1:H + 1 + step]
        near_y = ref[y, own, zs] + ref[y + 2, own, zs]
        blank = jnp.zeros((step, 128), f32)
        left = ref[y + 1, own, lo - 128:lo] if lo > 0 else blank
        right = ref[y + 1, own, lo + B:lo + B + 128] if lo + B < ref.shape[2] else blank
        wide = jnp.concatenate([left, c, right], axis=1)
        near_z = (pltpu.roll(wide, 1, 1) + pltpu.roll(wide, B + 255, 1))[:, 128:128 + B]
        twice = 2.0 * c
        stencil = (
            cx[here, :] * (twice - near_x) + cys[y] * (twice - near_y) + cz[0:1, zs] * (twice - near_z)
        )
        return rhs[y, here, zs] - (shift_term * c + rho[y, here, zs] * stencil)

    def inverse_diagonal(rho, cx, cys, cz, y, k, r, step):
        zs = slice(k * B, k * B + B)
        here = pl.ds(r, step)
        return 1.0 / (shift_term + 2.0 * rho[y, here, zs] * (cx[here, :] + cys[y] + cz[0:1, zs]))

    square = (n, n)
    diag = lax.broadcasted_iota(jnp.int32, square, 0) == lax.broadcasted_iota(jnp.int32, square, 1)
    column = jnp.sum(jnp.where(diag, jnp.broadcast_to(sx_ref[...], square), 0.0), axis=1, keepdims=True)
    CX[...] = jnp.broadcast_to(column, (n, B))
    cy = [sy_ref[y] for y in range(ny)]
    cy1 = [(cy[2 * y] + cy[2 * y + 1]) * 0.125 for y in range(ny1)]

    neighbours = []

    def enter():
        pl.semaphore_wait(barrier, npx + npy + 2)
        neighbours.extend([
            push(CB.at[0], CB.at[1], xp, j, has_xp, has_xm),
            push(CB.at[0], CB.at[2], xm, j, has_xm, has_xp),
            push(CB.at[0], CB.at[3], i, yp, has_yp, has_ym),
            push(CB.at[0], CB.at[4], i, ym, has_ym, has_yp),
        ])

    def keep(value, y, rows, r, step):
        at = pl.ds(pl.multiple_of(y * rows + r, step), step)
        SH[at, :], SL[at, :] = split(value)

    def smooth_z(block, planes, rows):
        z = mm3((SH[0:planes * rows], SL[0:planes * rows]), split(block), True)
        return [z[y * rows:(y + 1) * rows] for y in range(planes)]

    def window(ref, y, k, width, side):
        lo = k * width
        parts = [ref[y, :, lo:lo + width]]
        blank = jnp.zeros((ref.shape[1], side), f32)
        parts.insert(0, ref[y, :, lo - side:lo] if lo > 0 else blank)
        parts.append(ref[y, :, lo + width:lo + width + side] if lo + width < ref.shape[2] else blank)
        return jnp.concatenate(parts, axis=1)

    own = slice(H, H + n)
    own1 = slice(H, H + n1)
    mean_x = weights((n1, n), 1, 0, 0, 0.5, 0.0)
    mean_z = weights((B, half), 0, 0, 0, 0.5, 0.0)

    def scaled_residual(ref, halos, target, blocks, k):
        arrive(halos[k])

        def body(r, step):
            for y in range(ny):
                v = residual(F, ref, RHO, CX, cy, sz_ref, y, k, r, step)
                target[y, pl.ds(pl.multiple_of(at0 + r, step), step), cols[k]] = v * RD[y, pl.ds(r, step), cols[k]]

        strips(n, body)
        blocks.append(to_block(target, at0, n, g, cols[k]))

    early = max(1, nk - 2)
    first_alone = [(0, 1), (1, nk)]

    halos, blocks = [], []
    for k in range(nk):
        for copy in parts[k]:
            copy.wait()

        def body(r, step, k=k):
            here = pl.ds(r, step)
            for y in range(ny):
                rd = inverse_diagonal(RHO, CX, cy, sz_ref, y, k, r, step)
                RD[y, here, cols[k]] = rd
                keep(F[y, here, cols[k]] * rd, y, n, r, step)

        strips(n, body)
        solved = smooth_z(LZ0[k], ny, n)
        for y in range(ny):
            UA[y + 1, own, cols[k]] = solved[y]
        if k == 0:
            enter()
        grouped(first_alone, B, k, halos, lambda zs: halo(UA, ny, n, zs))
        if k == early:
            scaled_residual(UA, halos, W, blocks, 0)
    for k in range(1, nk):
        scaled_residual(UA, halos, W, blocks, k)

    for copy in late:
        copy.wait()
    restrict_x = weights((n1, n + 2 * H), 1, H, 0, 0.375, 0.125)
    restrict_z = weights((B + 256, half), 0, 128, 0, 0.375, 0.125)
    CX1[...] = left_mul(mean_x, CX[...]) * 0.25
    for k in range(nk):
        fine_z = jnp.broadcast_to(sz_ref[:, cols[k]], (8, B))
        CZ1[:, k * half:k * half + half] = right_mul(fine_z, mean_z) * 0.25
        for y in range(ny1):
            pair = (RHO[2 * y, :, cols[k]] + RHO[2 * y + 1, :, cols[k]]) * 0.5
            RHO1[y, :, k * half:k * half + half] = right_mul(left_mul(mean_x, pair), mean_z)
    for y in range(ny1):
        for k in range(nk1):

            def body(r, step, y=y, k=k):
                RD1[y, pl.ds(r, step), cols[k]] = inverse_diagonal(RHO1, CX1, cy1, CZ1, y, k, r, step)

            strips(n1, body)

    lx0 = split(LX0[...])
    halos, rims, sides = [], [], []

    def fine_residual(k):
        arrive(halos[k])

        def body(r, step):
            for y in range(ny):
                v = residual(F, UB, RHO, CX, cy, sz_ref, y, k, r, step)
                R0[y, pl.ds(pl.multiple_of(r + H, H), step), cols[k]] = v

        strips(n, body)
        grouped([(0, nk - 1), (nk - 1, nk)], B, k, rims, lambda zs: halo_x(R0, (0, ny), n, zs))

    def restrict_rows(k):
        arrive(rims[k])
        for y in range(ny):
            TX[y, :, cols[k]] = left_mul(restrict_x, R0[y, :, cols[k]])

    def restrict_columns(k):
        zs = slice(k * half, k * half + half)
        for y in range(ny):
            T1[y + 1, :, zs] = right_mul(window(TX, y, k, B, 128), restrict_z)
        groups = [(0, nk - 2), (nk - 2, nk)]
        grouped(groups, half, k, sides, lambda at: halo_y(T1, ny, slice(None), at))

    def middle_rhs(k):
        arrive(sides[2 * k])
        arrive(sides[2 * k + 1])
        for y in range(ny1):
            a = 2 * y
            inner = T1[a + 1, :, cols[k]] + T1[a + 2, :, cols[k]]
            F1[y, :, cols[k]] = (T1[a, :, cols[k]] + 3.0 * inner + T1[a + 3, :, cols[k]]) * 0.125

    def middle_z(ref, before, rhs, k):

        def body(r, step):
            for y in range(ny1):
                keep(rhs(y, r, step) * RD1[y, pl.ds(r, step), cols[k]], y, n1, r, step)

        strips(n1, body)
        solved = smooth_z(LZ1[k], ny1, n1)
        for y in range(ny1):
            u = solved[y] if before is None else before[y + 1, own1, cols[k]] + solved[y]
            ref[y + 1, own1, cols[k]] = u

    def middle_first(k):
        middle_rhs(k)
        middle_z(M1, None, lambda y, r, step: F1[y, pl.ds(r, step), cols[k]], k)

    for k in range(nk):
        arrive(blocks[k])
        for y in range(ny):
            UB[y + 1, own, cols[k]] = UA[y + 1, own, cols[k]] + mm3(lx0, split(W[y, :, cols[k]]))
        grouped([(0, nk - 2), (nk - 2, nk - 1), (nk - 1, nk)], B, k, halos, lambda zs: halo(UB, ny, n, zs))
        if k == nk - 2:
            for m in range(nk - 2):
                fine_residual(m)
    fine_residual(nk - 2)
    fine_residual(nk - 1)
    for k in range(nk - 1):
        restrict_rows(k)
    for k in range(nk - 2):
        restrict_columns(k)
    restrict_rows(nk - 1)
    restrict_columns(nk - 2)
    restrict_columns(nk - 1)
    for k in range(nk1):
        middle_first(k)

    lx1 = split(LX1[...])

    whole = slice(None)

    def middle_x(ref, target, result):
        arrive(halo(ref, ny1, n1, whole))
        for k in range(nk1):

            def body(r, step, k=k):
                for y in range(ny1):
                    v = residual(F1, ref, RHO1, CX1, cy1, CZ1, y, k, r, step)
                    at = pl.ds(pl.multiple_of(at1 + r, step), step)
                    target[y, at, cols[k]] = v * RD1[y, pl.ds(r, step), cols[k]]

            strips(n1, body)
        arrive(to_block(target, at1, n1, g1, whole))
        for k in range(nk1):
            for y in range(ny1):
                solved = mm3(lx1, split(target[y, :, cols[k]]))
                result[y + 1, own1, cols[k]] = ref[y + 1, own1, cols[k]] + solved
        return halo(result, ny1, n1, whole)

    edges = middle_x(M1, V, M2)
    arrive(edges)

    total = jnp.zeros((1, B), f32)
    for k in range(nk1):
        step1 = min(n1, 32)

        def add(t, total, k=k, step1=step1):
            r = pl.multiple_of(t * step1, step1)
            for y in range(ny1):
                v = residual(F1, M2, RHO1, CX1, cy1, CZ1, y, k, r, step1)
                total = total + jnp.sum(v, axis=0, keepdims=True)
            return total

        total = lax.fori_loop(0, n1 // step1, add, total)
    mean = jnp.sum(total, axis=1, keepdims=True) * (1.0 / (ny1 * n1 * nz1))
    lane = lax.broadcasted_iota(jnp.int32, CB.shape[1:], 1)
    G1[i] = jnp.where(lane == j * npx + i, mean, 0.0)
    arrive([push(G1.at[i], G1.at[i], lax.rem(i + s, npx), j) for s in range(1, npx)])
    G2[j] = jnp.sum(G1[...], axis=0)
    arrive([push(G2.at[j], G2.at[j], i, lax.rem(j + s, npy)) for s in range(1, npy)])
    means = jnp.sum(G2[...], axis=0)[0:1]
    arrive(neighbours)
    e = [jnp.sum(CB[s][0:1] * means, axis=1, keepdims=True) for s in range(5)]
    MP[1:ny1 + 1, own1, :] = M2[1:ny1 + 1, own1, :] + e[0]
    MP[1:ny1 + 1, 0:H, :] = M2[1:ny1 + 1, 0:H, :] + e[1]
    MP[1:ny1 + 1, n1 + H:n1 + 2 * H, :] = M2[1:ny1 + 1, n1 + H:n1 + 2 * H, :] + e[2]
    MP[0, own1, :] = M2[0, own1, :] + e[3]
    MP[ny1 + 1, own1, :] = M2[ny1 + 1, own1, :] + e[4]

    for k in range(nk1):

        def rhs(y, r, step, k=k):
            return residual(F1, MP, RHO1, CX1, cy1, CZ1, y, k, r, step)

        middle_z(M3, MP, rhs, k)
    edges = middle_x(M3, V2, M4) + halo_corners(M4, ny1, n1, whole)

    raise_x = weights((n + 2 * H, n1 + 2 * H), 0, H, H, 0.75, 0.25)
    raise_z = weights((half + 256, B), 1, 0, 128, 0.75, 0.25)
    row = lax.broadcasted_iota(jnp.int32, (n + 2 * H, 1), 0)
    inside = jnp.logical_and(jnp.logical_or(row >= H, has_xm), jnp.logical_or(row < n + H, has_xp))
    arrive(edges)

    def prolong(k):
        zs = cols[k]
        rows = n1 + 2 * H
        wide = right_mul(jnp.concatenate([window(M4, y, k, half, 128) for y in range(ny1 + 2)], axis=0), raise_z)
        raised = [left_mul(raise_x, wide[y * rows:(y + 1) * rows]) for y in range(ny1 + 2)]
        for y in range(ny + 2):
            near = (y - 1) // 2 + 1
            other = near - 1 if (y - 1) % 2 == 0 else near + 1
            c = (3.0 * raised[near] + raised[other]) * 0.25
            if y == 0:
                UC[0, own, zs] = jnp.where(has_ym, UB[0, own, zs] + c[own], 0.0)
            elif y == ny + 1:
                UC[y, own, zs] = jnp.where(has_yp, UB[y, own, zs] + c[own], 0.0)
            else:
                UC[y, :, zs] = jnp.where(inside, UB[y, :, zs] + c, 0.0)

    halos, blocks = [], []
    prolong(0)
    for k in range(nk):
        if k + 1 < nk:
            prolong(k + 1)

        def body(r, step, k=k):
            for y in range(ny):
                v = residual(F, UC, RHO, CX, cy, sz_ref, y, k, r, step)
                keep(v * RD[y, pl.ds(r, step), cols[k]], y, n, r, step)

        strips(n, body)
        solved = smooth_z(LZ0[k], ny, n)
        for y in range(ny):
            UD[y + 1, own, cols[k]] = UC[y + 1, own, cols[k]] + solved[y]
        grouped(first_alone, B, k, halos, lambda zs: halo(UD, ny, n, zs))
        if k == early:
            scaled_residual(UD, halos, W2, blocks, 0)
    before = len(pending)
    for k in range(1, nk):
        scaled_residual(UD, halos, W2, blocks, k)
    drain(before - (g - 1))
    lx0 = split(LX0[...])
    stores = []
    for k in range(nk):
        arrive(blocks[k])
        for y in range(ny):
            OUT[y, :, cols[k]] = UD[y + 1, own, cols[k]] + mm3(lx0, split(W2[y, :, cols[k]]))
            store = pltpu.make_async_copy(OUT.at[y, :, cols[k]], out_ref.at[:, y, cols[k]], ls.at[len(stores)])
            store.start()
            stores.append(store)
    drain(len(pending))
    for store in stores:
        store.wait()


def per_device(npx, npy, f, rho, sx, sy, sz, lz0, lx0, lz1, lx1, c):
    n, ny, nz = f.shape
    B = lz0.shape[-1]
    n1, ny1, nz1 = n // 2, ny // 2, nz // 2
    g, g1, nk = B // n, B // n1, nz // B
    lanes = -(-c.shape[1] // 128) * 128
    fine = pltpu.VMEM((ny, n, nz), f32)
    padded = pltpu.VMEM((ny + 2, n + 2 * H, nz), f32)
    coarse = pltpu.VMEM((ny1, n1, nz1), f32)
    coarse_padded = pltpu.VMEM((ny1 + 2, n1 + 2 * H, nz1), f32)
    copies = 4 + nk * (14 + 2 * g) + nk // 2 * (18 + 2 * g1) + npx + npy - 2
    anywhere = pl.BlockSpec(memory_space=pl.ANY)
    vmem = pl.BlockSpec(memory_space=pltpu.VMEM)
    smem = pl.BlockSpec(memory_space=pltpu.SMEM)
    return pl.pallas_call(
        functools.partial(kernel, (n, ny, nz, B, npx, npy)),
        out_shape=jax.ShapeDtypeStruct(f.shape, f32),
        in_specs=[anywhere, anywhere, vmem, smem, vmem, anywhere, anywhere, anywhere, anywhere, vmem],
        out_specs=anywhere,
        scratch_shapes=[
            fine, fine, fine, padded, padded, padded, padded,
            pltpu.VMEM((ny, B, nz), f32), pltpu.VMEM((ny, B, nz), f32),
            pltpu.VMEM((ny, n + 2 * H, nz), f32), pltpu.VMEM((ny, n1, nz), f32), pltpu.VMEM((ny + 2, n1, nz1), f32),
            coarse, coarse, coarse,
            coarse_padded, coarse_padded, coarse_padded, coarse_padded, coarse_padded,
            pltpu.VMEM((ny1, B, nz1), f32), pltpu.VMEM((ny1, B, nz1), f32),
            pltpu.VMEM((npx, 8, lanes), f32), pltpu.VMEM((npy, 8, lanes), f32), pltpu.VMEM((5, 8, lanes), f32),
            pltpu.VMEM((n, B), f32), pltpu.VMEM((n1, B), f32), pltpu.VMEM((8, nz1), f32),
            pltpu.VMEM(lz0.shape, f32), pltpu.VMEM(lz1.shape, f32),
            pltpu.VMEM((n, B), f32), pltpu.VMEM((n1, B), f32),
            pltpu.VMEM((ny * n, B), bf16), pltpu.VMEM((ny * n, B), bf16), fine,
            pltpu.SemaphoreType.DMA((copies,)), pltpu.SemaphoreType.DMA((copies,)),
            pltpu.SemaphoreType.DMA((nk * (2 * ny + 1) + 3,)),
        ],
        compiler_params=pltpu.CompilerParams(
            collective_id=0, has_side_effects=True, vmem_limit_bytes=56 * 1024 * 1024
        ),
    )(f, rho, sx.reshape(1, n), sy, sz.reshape(1, nz), lz0, lx0, lz1, lx1, c)


def solution(mesh):
    placed = (
        P("px", "py", None), P("px", "py", None), P("px"), P("py"),
        P(), P(), P(), P(), P(), P(("py", "px"), None),
    )
    body = functools.partial(per_device, mesh.shape["px"], mesh.shape["py"])
    return jax.shard_map(
        body, mesh=mesh, in_specs=placed, out_specs=P("px", "py", None), check_vma=False
    )
```

```python
import functools

import jax
import jax.numpy as jnp
from jax import lax
from jax.experimental import pallas as pl
from jax.experimental.pallas import tpu as pltpu
from jax.sharding import PartitionSpec as P

f32 = jnp.float32
bf16 = jnp.bfloat16
MESH = pl.DeviceIdType.MESH
shift_term = 0.1
H = 8


def split(a):
    hi = a.astype(bf16)
    return hi, (a - hi.astype(f32)).astype(bf16)


def mm(a, b, transposed=False):
    dims = (((1,), (1 if transposed else 0,)), ((), ()))
    return lax.dot_general(a, b, dims, preferred_element_type=f32)


def mm3(a, b, transposed=False):
    (ah, al), (bh, bl) = a, b
    return mm(ah, bh, transposed) + (mm(ah, bl, transposed) + mm(al, bh, transposed))


def weights(shape, fine_dim, fine_pad, coarse_pad, inner, outer):
    fine = lax.broadcasted_iota(jnp.int32, shape, fine_dim) - fine_pad
    coarse = lax.broadcasted_iota(jnp.int32, shape, 1 - fine_dim) - coarse_pad
    d = fine - 2 * coarse
    near = jnp.where((d == 0) | (d == 1), inner, 0.0)
    if outer:
        near = jnp.where((d == -1) | (d == 2), outer, near)
    return near.astype(bf16)


def left_mul(m, v):
    hi, lo = split(v)
    return mm(m, hi) + mm(m, lo)


def right_mul(v, m):
    hi, lo = split(v)
    return mm(hi, m) + mm(lo, m)


def kernel(
    dims,
    f_in, rho_in, sx_ref, sy_ref, sz_ref, lz0_in, lx0_in, lz1_in, lx1_in, c_ref,
    out_ref,
    F, RHO, RD, UA, UB, UC, UD, W, W2, R0, TX, T1, F1, RHO1, RD1,
    M1, M2, MP, M3, M4, V, V2, G1, G2, CB, CX, CX1, CZ1, LZ0, LZ1, LX0, LX1, FS, RS,
    ss, rs, ls,
):
    n, ny, nz, B, npx, npy = dims
    n1, ny1, nz1 = n // 2, ny // 2, nz // 2
    nk, nk1 = nz // B, nz1 // B
    g, g1 = B // n, B // n1
    i, j = lax.axis_index("px"), lax.axis_index("py")
    has_xm, has_xp = i > 0, i < npx - 1
    has_ym, has_yp = j > 0, j < npy - 1
    xm, xp = lax.rem(i + npx - 1, npx), lax.rem(i + 1, npx)
    ym, yp = lax.rem(j + npy - 1, npy), lax.rem(j + 1, npy)

    loads = []

    def load(src, dst):
        copy = pltpu.make_async_copy(src, dst, ls.at[len(loads)])
        copy.start()
        loads.append(copy)
        return copy

    half = B // 2
    cols = [slice(k * B, k * B + B) for k in range(nk)]
    tiles = nz // 128
    first_loads = [load(rho_in, RS), load(f_in, FS), load(lz0_in, LZ0)]

    def rows_of(y, tile):
        return pl.ds(tile * ny + y, n, stride=tiles * ny)
    at0 = pl.multiple_of(lax.rem(i, g) * n, n)
    at1 = pl.multiple_of(lax.rem(i, g1) * n1, n1)
    late = [
        load(lx0_in.at[i // g, pl.ds(at0, n), :], LX0),
        load(lx1_in.at[i // g1, pl.ds(at1, n1), :], LX1),
        load(lz1_in, LZ1),
    ]

    for ref in (UA, UB, UD, R0, M1, M2, M3, M4):
        rows = ref.shape[1]

        @pl.when(jnp.logical_not(has_xm))
        def _(ref=ref):
            ref[:, 0:H, :] = jnp.zeros((ref.shape[0], H, ref.shape[2]), f32)

        @pl.when(jnp.logical_not(has_xp))
        def _(ref=ref, rows=rows):
            ref[:, rows - H:rows, :] = jnp.zeros((ref.shape[0], H, ref.shape[2]), f32)

    for ref in (UA, UB, UD, T1, M1, M2, M3, M4):
        planes = ref.shape[0]

        @pl.when(jnp.logical_not(has_ym))
        def _(ref=ref):
            ref[0] = jnp.zeros(ref.shape[1:], f32)

        @pl.when(jnp.logical_not(has_yp))
        def _(ref=ref, planes=planes):
            ref[planes - 1] = jnp.zeros(ref.shape[1:], f32)

    count = c_ref.shape[1]
    CB[...] = jnp.zeros(CB.shape, f32)
    CB[0, :, 0:count] = jnp.broadcast_to(c_ref[...], (8, count))

    barrier = pltpu.get_barrier_semaphore()
    for s in range(1, npx):
        pl.semaphore_signal(barrier, inc=1, device_id={"px": lax.rem(i + s, npx), "py": j}, device_id_type=MESH)
    for s in range(1, npy):
        pl.semaphore_signal(barrier, inc=1, device_id={"px": i, "py": lax.rem(j + s, npy)}, device_id_type=MESH)
    for to_x in (xm, xp):
        for to_y in (ym, yp):
            pl.semaphore_signal(barrier, inc=1, device_id={"px": to_x, "py": to_y}, device_id_type=MESH)

    pending = []

    def push(src, dst, to_x, to_y, sends=None, receives=None):
        at = len(pending)
        copy = pltpu.make_async_remote_copy(
            src_ref=src, dst_ref=dst, send_sem=ss.at[at], recv_sem=rs.at[at],
            device_id={"px": to_x, "py": to_y}, device_id_type=MESH,
        )
        if sends is None:
            copy.start()
        else:
            pl.when(sends)(copy.start)
        pending.append((sends, copy))
        return receives, copy

    def arrive(handles):
        for receives, copy in handles:
            if receives is None:
                copy.wait_recv()
            else:
                pl.when(receives)(copy.wait_recv)

    def sent(sends, copy):
        if sends is None:
            copy.wait_send()
        else:
            pl.when(sends)(copy.wait_send)

    def halo_x(ref, planes, rows, zs):
        a, b = planes
        return [
            push(ref.at[a:b, rows:rows + H, zs], ref.at[a:b, 0:H, zs], xp, j, has_xp, has_xm),
            push(ref.at[a:b, H:2 * H, zs], ref.at[a:b, rows + H:rows + 2 * H, zs], xm, j, has_xm, has_xp),
        ]

    def halo_y(ref, planes, r, zs):
        return [
            push(ref.at[planes, r, zs], ref.at[0, r, zs], i, yp, has_yp, has_ym),
            push(ref.at[1, r, zs], ref.at[planes + 1, r, zs], i, ym, has_ym, has_yp),
        ]

    def halo(ref, planes, rows, zs):
        return halo_y(ref, planes, slice(H, H + rows), zs) + halo_x(ref, (1, planes + 1), rows, zs)

    def halo_corners(ref, planes, rows, zs):
        both = jnp.logical_and
        low, high = slice(0, H), slice(rows + H, rows + 2 * H)
        first, last = slice(H, 2 * H), slice(rows, rows + H)
        return [
            push(ref.at[planes, last, zs], ref.at[0, low, zs], xp, yp, both(has_xp, has_yp), both(has_xm, has_ym)),
            push(ref.at[1, last, zs], ref.at[planes + 1, low, zs], xp, ym, both(has_xp, has_ym), both(has_xm, has_yp)),
            push(ref.at[planes, first, zs], ref.at[0, high, zs], xm, yp, both(has_xm, has_yp), both(has_xp, has_ym)),
            push(ref.at[1, first, zs], ref.at[planes + 1, high, zs], xm, ym, both(has_xm, has_ym), both(has_xp, has_yp)),
        ]

    def to_block(ref, at, rows, peers, zs):
        here = lax.rem(i, peers)
        base = i - here
        mine = ref.at[:, pl.ds(at, rows), zs]
        return [push(mine, mine, base + lax.rem(here + s, peers), j) for s in range(1, peers)]

    def residual(rhs, ref, rho, cx, cys, cz, y, k):
        rows = rhs.shape[1]
        lo = k * B
        zs = slice(lo, lo + B)
        own = slice(H, H + rows)
        c = ref[y + 1, own, zs]
        near_x = ref[y + 1, H - 1:H - 1 + rows, zs] + ref[y + 1, H + 1:H + 1 + rows, zs]
        near_y = ref[y, own, zs] + ref[y + 2, own, zs]
        blank = jnp.zeros((rows, 128), f32)
        left = ref[y + 1, own, lo - 128:lo] if lo > 0 else blank
        right = ref[y + 1, own, lo + B:lo + B + 128] if lo + B < ref.shape[2] else blank
        wide = jnp.concatenate([left, c, right], axis=1)
        near_z = (pltpu.roll(wide, 1, 1) + pltpu.roll(wide, B + 255, 1))[:, 128:128 + B]
        twice = 2.0 * c
        stencil = cx[...] * (twice - near_x) + cys[y] * (twice - near_y) + cz[0:1, zs] * (twice - near_z)
        return rhs[y, :, zs] - (shift_term * c + rho[y, :, zs] * stencil)

    def inverse_diagonal(rho, cx, cys, cz, y, k):
        zs = slice(k * B, k * B + B)
        return 1.0 / (shift_term + 2.0 * rho[y, :, zs] * (cx[...] + cys[y] + cz[0:1, zs]))

    square = (n, n)
    diag = lax.broadcasted_iota(jnp.int32, square, 0) == lax.broadcasted_iota(jnp.int32, square, 1)
    column = jnp.sum(jnp.where(diag, jnp.broadcast_to(sx_ref[...], square), 0.0), axis=1, keepdims=True)
    CX[...] = jnp.broadcast_to(column, (n, B))
    cy = [sy_ref[y] for y in range(ny)]
    cy1 = [(cy[2 * y] + cy[2 * y + 1]) * 0.125 for y in range(ny1)]

    neighbours = []

    def enter():
        pl.semaphore_wait(barrier, npx + npy + 2)
        neighbours.extend([
            push(CB.at[0], CB.at[1], xp, j, has_xp, has_xm),
            push(CB.at[0], CB.at[2], xm, j, has_xm, has_xp),
            push(CB.at[0], CB.at[3], i, yp, has_yp, has_ym),
            push(CB.at[0], CB.at[4], i, ym, has_ym, has_yp),
        ])

    def smooth_z(values, block, planes, rows):
        w = jnp.concatenate(values, axis=0)
        z = mm3(split(w), split(block), True)
        return [z[y * rows:(y + 1) * rows] for y in range(planes)]

    def window(ref, y, k, width, side):
        lo = k * width
        parts = [ref[y, :, lo:lo + width]]
        blank = jnp.zeros((ref.shape[1], side), f32)
        parts.insert(0, ref[y, :, lo - side:lo] if lo > 0 else blank)
        parts.append(ref[y, :, lo + width:lo + width + side] if lo + width < ref.shape[2] else blank)
        return jnp.concatenate(parts, axis=1)

    own = slice(H, H + n)
    own1 = slice(H, H + n1)
    mean_x = weights((n1, n), 1, 0, 0, 0.5, 0.0)
    mean_z = weights((B, half), 0, 0, 0, 0.5, 0.0)

    def scaled_residual(ref, halos, target, blocks, k):
        arrive(halos[k])
        for y in range(ny):
            r = residual(F, ref, RHO, CX, cy, sz_ref, y, k)
            target[y, pl.ds(at0, n), cols[k]] = r * RD[y, :, cols[k]]
        blocks.append(to_block(target, at0, n, g, cols[k]))

    halos, blocks = [], []
    for k in range(nk + 1):
        if k < nk:
            if k == 0:
                for copy in first_loads:
                    copy.wait()
            for tile in range(k * B // 128, (k + 1) * B // 128):
                for y in range(ny):
                    F[y, :, tile * 128:tile * 128 + 128] = FS[rows_of(y, tile), :]
                    RHO[y, :, tile * 128:tile * 128 + 128] = RS[rows_of(y, tile), :]
            scaled = []
            for y in range(ny):
                rd = inverse_diagonal(RHO, CX, cy, sz_ref, y, k)
                RD[y, :, cols[k]] = rd
                scaled.append(F[y, :, cols[k]] * rd)
            solved = smooth_z(scaled, LZ0[k], ny, n)
            for y in range(ny):
                UA[y + 1, own, cols[k]] = solved[y]
            if k == 0:
                enter()
            halos.append(halo(UA, ny, n, cols[k]))
        if k > 0:
            scaled_residual(UA, halos, W, blocks, k - 1)

    for copy in late:
        copy.wait()
    restrict_x = weights((n1, n + 2 * H), 1, H, 0, 0.375, 0.125)
    restrict_z = weights((B + 256, half), 0, 128, 0, 0.375, 0.125)
    CX1[...] = left_mul(mean_x, CX[...]) * 0.25
    for k in range(nk):
        fine_z = jnp.broadcast_to(sz_ref[:, cols[k]], (8, B))
        CZ1[:, k * half:k * half + half] = right_mul(fine_z, mean_z) * 0.25
        for y in range(ny1):
            pair = (RHO[2 * y, :, cols[k]] + RHO[2 * y + 1, :, cols[k]]) * 0.5
            RHO1[y, :, k * half:k * half + half] = right_mul(left_mul(mean_x, pair), mean_z)
    for y in range(ny1):
        for k in range(nk1):
            RD1[y, :, cols[k]] = inverse_diagonal(RHO1, CX1, cy1, CZ1, y, k)

    lx0 = split(LX0[...])
    halos, rims, sides, halos1 = [], [], [], []

    def fine_residual(k):
        arrive(halos[k])
        for y in range(ny):
            R0[y, own, cols[k]] = residual(F, UB, RHO, CX, cy, sz_ref, y, k)
        rims.append(halo_x(R0, (0, ny), n, cols[k]))

    def restrict_rows(k):
        arrive(rims[k])
        for y in range(ny):
            TX[y, :, cols[k]] = left_mul(restrict_x, R0[y, :, cols[k]])

    def restrict_columns(k):
        zs = slice(k * half, k * half + half)
        for y in range(ny):
            T1[y + 1, :, zs] = right_mul(window(TX, y, k, B, 128), restrict_z)
        sides.append(halo_y(T1, ny, slice(None), zs))

    def middle_rhs(k):
        arrive(sides[2 * k])
        arrive(sides[2 * k + 1])
        for y in range(ny1):
            a = 2 * y
            inner = T1[a + 1, :, cols[k]] + T1[a + 2, :, cols[k]]
            F1[y, :, cols[k]] = (T1[a, :, cols[k]] + 3.0 * inner + T1[a + 3, :, cols[k]]) * 0.125

    def middle_z(ref, before, rhs, k):
        scaled = [r * RD1[y, :, cols[k]] for y, r in enumerate(rhs)]
        solved = smooth_z(scaled, LZ1[k], ny1, n1)
        for y in range(ny1):
            u = solved[y] if before is None else before[y + 1, own1, cols[k]] + solved[y]
            ref[y + 1, own1, cols[k]] = u
        return halo(ref, ny1, n1, cols[k])

    def middle_first(k):
        middle_rhs(k)
        halos1.append(middle_z(M1, None, [F1[y, :, cols[k]] for y in range(ny1)], k))

    for k in range(nk):
        arrive(blocks[k])
        for y in range(ny):
            UB[y + 1, own, cols[k]] = UA[y + 1, own, cols[k]] + mm3(lx0, split(W[y, :, cols[k]]))
        halos.append(halo(UB, ny, n, cols[k]))
        if k >= 1:
            fine_residual(k - 1)
            restrict_rows(k - 1)
        if k >= 2:
            restrict_columns(k - 2)
    fine_residual(nk - 1)
    for k in range(nk1 - 1):
        middle_first(k)
    restrict_rows(nk - 1)
    restrict_columns(nk - 2)
    restrict_columns(nk - 1)
    middle_first(nk1 - 1)

    lx1 = split(LX1[...])

    def middle_x(ref, halos1, target, result, diagonals):
        sent = []
        for k in range(nk1):
            arrive(halos1[k])
            for y in range(ny1):
                r = residual(F1, ref, RHO1, CX1, cy1, CZ1, y, k)
                target[y, pl.ds(at1, n1), cols[k]] = r * RD1[y, :, cols[k]]
            sent.append(to_block(target, at1, n1, g1, cols[k]))
        edges = []
        for k in range(nk1):
            arrive(sent[k])
            for y in range(ny1):
                solved = mm3(lx1, split(target[y, :, cols[k]]))
                result[y + 1, own1, cols[k]] = ref[y + 1, own1, cols[k]] + solved
            edge = halo(result, ny1, n1, cols[k])
            if diagonals:
                edge = edge + halo_corners(result, ny1, n1, cols[k])
            edges.append(edge)
        return edges

    edges = middle_x(M1, halos1, V, M2, False)

    total = jnp.zeros((1, B), f32)
    for k in range(nk1):
        arrive(edges[k])
        for y in range(ny1):
            r = residual(F1, M2, RHO1, CX1, cy1, CZ1, y, k)
            total = total + jnp.sum(r, axis=0, keepdims=True)
    mean = jnp.sum(total, axis=1, keepdims=True) * (1.0 / (ny1 * n1 * nz1))
    lane = lax.broadcasted_iota(jnp.int32, CB.shape[1:], 1)
    G1[i] = jnp.where(lane == j * npx + i, mean, 0.0)
    arrive([push(G1.at[i], G1.at[i], lax.rem(i + s, npx), j) for s in range(1, npx)])
    G2[j] = jnp.sum(G1[...], axis=0)
    arrive([push(G2.at[j], G2.at[j], i, lax.rem(j + s, npy)) for s in range(1, npy)])
    means = jnp.sum(G2[...], axis=0)[0:1]
    arrive(neighbours)
    e = [jnp.sum(CB[s][0:1] * means, axis=1, keepdims=True) for s in range(5)]
    MP[1:ny1 + 1, own1, :] = M2[1:ny1 + 1, own1, :] + e[0]
    MP[1:ny1 + 1, 0:H, :] = M2[1:ny1 + 1, 0:H, :] + e[1]
    MP[1:ny1 + 1, n1 + H:n1 + 2 * H, :] = M2[1:ny1 + 1, n1 + H:n1 + 2 * H, :] + e[2]
    MP[0, own1, :] = M2[0, own1, :] + e[3]
    MP[ny1 + 1, own1, :] = M2[ny1 + 1, own1, :] + e[4]

    halos1 = []
    for k in range(nk1):
        rhs = [residual(F1, MP, RHO1, CX1, cy1, CZ1, y, k) for y in range(ny1)]
        halos1.append(middle_z(M3, MP, rhs, k))
    edges = middle_x(M3, halos1, V2, M4, True)

    raise_x = weights((n + 2 * H, n1 + 2 * H), 0, H, H, 0.75, 0.25)
    raise_z = weights((half + 256, B), 1, 0, 128, 0.75, 0.25)
    row = lax.broadcasted_iota(jnp.int32, (n + 2 * H, 1), 0)
    inside = jnp.logical_and(jnp.logical_or(row >= H, has_xm), jnp.logical_or(row < n + H, has_xp))
    arrived = []

    def prolong(k):
        while len(arrived) < min(k + 1, nk - 1) // 2 + 1:
            arrive(edges[len(arrived)])
            arrived.append(k)
        zs = cols[k]
        raised = [left_mul(raise_x, right_mul(window(M4, y, k, half, 128), raise_z)) for y in range(ny1 + 2)]
        for y in range(ny + 2):
            near = (y - 1) // 2 + 1
            other = near - 1 if (y - 1) % 2 == 0 else near + 1
            c = (3.0 * raised[near] + raised[other]) * 0.25
            if y == 0:
                UC[0, own, zs] = jnp.where(has_ym, UB[0, own, zs] + c[own], 0.0)
            elif y == ny + 1:
                UC[y, own, zs] = jnp.where(has_yp, UB[y, own, zs] + c[own], 0.0)
            else:
                UC[y, :, zs] = jnp.where(inside, UB[y, :, zs] + c, 0.0)

    settled = len(pending)
    halos, blocks = [], []
    prolong(0)
    for k in range(nk + 1):
        if k + 1 < nk:
            prolong(k + 1)
        if k < nk:
            scaled = [residual(F, UC, RHO, CX, cy, sz_ref, y, k) * RD[y, :, cols[k]] for y in range(ny)]
            solved = smooth_z(scaled, LZ0[k], ny, n)
            for y in range(ny):
                UD[y + 1, own, cols[k]] = UC[y + 1, own, cols[k]] + solved[y]
            halos.append(halo(UD, ny, n, cols[k]))
        if k > 0:
            scaled_residual(UD, halos, W2, blocks, k - 1)
    lx0 = split(LX0[...])
    for sends, copy in pending[:settled]:
        sent(sends, copy)
    for k in range(nk):
        arrive(blocks[k])
        for y in range(ny):
            result = UD[y + 1, own, cols[k]] + mm3(lx0, split(W2[y, :, cols[k]]))
            for t in range(B // 128):
                FS[rows_of(y, k * B // 128 + t), :] = result[:, t * 128:t * 128 + 128]
    store = pltpu.make_async_copy(FS, out_ref, ls.at[0])
    store.start()
    for sends, copy in pending[settled:]:
        sent(sends, copy)
    store.wait()


def per_device(npx, npy, f, rho, sx, sy, sz, lz0, lx0, lz1, lx1, c):
    n, ny, nz = f.shape
    B = lz0.shape[-1]
    n1, ny1, nz1 = n // 2, ny // 2, nz // 2
    g, g1, nk = B // n, B // n1, nz // B
    lanes = -(-c.shape[1] // 128) * 128
    linear = pltpu.VMEM((n * nz // 128 * ny, 128), f32)
    fine = pltpu.VMEM((ny, n, nz), f32)
    padded = pltpu.VMEM((ny + 2, n + 2 * H, nz), f32)
    coarse = pltpu.VMEM((ny1, n1, nz1), f32)
    coarse_padded = pltpu.VMEM((ny1 + 2, n1 + 2 * H, nz1), f32)
    copies = 4 + nk * (14 + 2 * g) + nk // 2 * (18 + 2 * g1) + npx + npy - 2

    def rows(field):
        return field.reshape(n, ny, nz // 128, 128).transpose(0, 2, 1, 3).reshape(-1, 128)

    anywhere = pl.BlockSpec(memory_space=pl.ANY)
    vmem = pl.BlockSpec(memory_space=pltpu.VMEM)
    smem = pl.BlockSpec(memory_space=pltpu.SMEM)
    out = pl.pallas_call(
        functools.partial(kernel, (n, ny, nz, B, npx, npy)),
        out_shape=jax.ShapeDtypeStruct((n * nz // 128 * ny, 128), f32),
        in_specs=[anywhere, anywhere, vmem, smem, vmem, anywhere, anywhere, anywhere, anywhere, vmem],
        out_specs=anywhere,
        scratch_shapes=[
            fine, fine, fine, padded, padded, padded, padded,
            pltpu.VMEM((ny, B, nz), f32), pltpu.VMEM((ny, B, nz), f32),
            pltpu.VMEM((ny, n + 2 * H, nz), f32), pltpu.VMEM((ny, n1, nz), f32), pltpu.VMEM((ny + 2, n1, nz1), f32),
            coarse, coarse, coarse,
            coarse_padded, coarse_padded, coarse_padded, coarse_padded, coarse_padded,
            pltpu.VMEM((ny1, B, nz1), f32), pltpu.VMEM((ny1, B, nz1), f32),
            pltpu.VMEM((npx, 8, lanes), f32), pltpu.VMEM((npy, 8, lanes), f32), pltpu.VMEM((5, 8, lanes), f32),
            pltpu.VMEM((n, B), f32), pltpu.VMEM((n1, B), f32), pltpu.VMEM((8, nz1), f32),
            pltpu.VMEM(lz0.shape, f32), pltpu.VMEM(lz1.shape, f32),
            pltpu.VMEM((n, B), f32), pltpu.VMEM((n1, B), f32), linear, linear,
            pltpu.SemaphoreType.DMA((copies,)), pltpu.SemaphoreType.DMA((copies,)),
            pltpu.SemaphoreType.DMA((6,)),
        ],
        compiler_params=pltpu.CompilerParams(
            collective_id=0, has_side_effects=True, vmem_limit_bytes=56 * 1024 * 1024
        ),
    )(rows(f), rows(rho), sx.reshape(1, n), sy, sz.reshape(1, nz), lz0, lx0, lz1, lx1, c)
    return out.reshape(n, nz // 128, ny, 128).transpose(0, 2, 1, 3).reshape(n, ny, nz)


def solution(mesh):
    placed = (
        P("px", "py", None), P("px", "py", None), P("px"), P("py"),
        P(), P(), P(), P(), P(), P(("py", "px"), None),
    )
    body = functools.partial(per_device, mesh.shape["px"], mesh.shape["py"])
    return jax.shard_map(
        body, mesh=mesh, in_specs=placed, out_specs=P("px", "py", None), check_vma=False
    )
```

```python
import functools

import jax
import jax.numpy as jnp
from jax import lax
from jax.experimental import pallas as pl
from jax.experimental.pallas import tpu as pltpu
from jax.sharding import PartitionSpec as P

f32 = jnp.float32
bf16 = jnp.bfloat16
MESH = pl.DeviceIdType.MESH
shift_term = 0.1
H = 8


def split(a):
    hi = a.astype(bf16)
    return hi, (a - hi.astype(f32)).astype(bf16)


def mm(a, b, transposed=False):
    dims = (((1,), (1 if transposed else 0,)), ((), ()))
    return lax.dot_general(a, b, dims, preferred_element_type=f32)


def mm3(a, b, transposed=False):
    (ah, al), (bh, bl) = a, b
    return mm(ah, bh, transposed) + (mm(ah, bl, transposed) + mm(al, bh, transposed))


def weights(shape, fine_dim, fine_pad, coarse_pad, inner, outer):
    fine = lax.broadcasted_iota(jnp.int32, shape, fine_dim) - fine_pad
    coarse = lax.broadcasted_iota(jnp.int32, shape, 1 - fine_dim) - coarse_pad
    d = fine - 2 * coarse
    near = jnp.where((d == 0) | (d == 1), inner, 0.0)
    if outer:
        near = jnp.where((d == -1) | (d == 2), outer, near)
    return near.astype(bf16)


def left_mul(m, v):
    hi, lo = split(v)
    return mm(m, hi) + mm(m, lo)


def right_mul(v, m):
    hi, lo = split(v)
    return mm(hi, m) + mm(lo, m)


def kernel(
    dims,
    f_in, rho_in, sx_ref, sy_ref, sz_ref, lz0_in, lx0_in, lz1_in, lx1_in, c_ref,
    out_ref,
    F, RHO, RD, UA, UB, UC, UD, W, W2, R0, TX, T1, F1, RHO1, RD1,
    M1, M2, MP, M3, M4, V, V2, G1, G2, CB, CX, CX1, CZ1, LZ0, LZ1, LX0, LX1, FS, RS,
    ss, rs, ls,
):
    n, ny, nz, B, npx, npy = dims
    n1, ny1, nz1 = n // 2, ny // 2, nz // 2
    nk, nk1 = nz // B, nz1 // B
    g, g1 = B // n, B // n1
    i, j = lax.axis_index("px"), lax.axis_index("py")
    has_xm, has_xp = i > 0, i < npx - 1
    has_ym, has_yp = j > 0, j < npy - 1
    xm, xp = lax.rem(i + npx - 1, npx), lax.rem(i + 1, npx)
    ym, yp = lax.rem(j + npy - 1, npy), lax.rem(j + 1, npy)

    loads = []

    def load(src, dst):
        copy = pltpu.make_async_copy(src, dst, ls.at[len(loads)])
        copy.start()
        loads.append(copy)
        return copy

    half = B // 2
    cols = [slice(k * B, k * B + B) for k in range(nk)]
    tiles = nz // 128
    first_loads = [load(rho_in, RS), load(f_in, FS), load(lz0_in, LZ0)]

    def rows_of(y, tile):
        return pl.ds(tile * ny + y, n, stride=tiles * ny)
    at0 = pl.multiple_of(lax.rem(i, g) * n, n)
    at1 = pl.multiple_of(lax.rem(i, g1) * n1, n1)
    late = [
        load(lx0_in.at[i // g, pl.ds(at0, n), :], LX0),
        load(lx1_in.at[i // g1, pl.ds(at1, n1), :], LX1),
        load(lz1_in, LZ1),
    ]

    for ref in (UA, UB, UD, R0, M1, M2, M3, M4):
        rows = ref.shape[1]

        @pl.when(jnp.logical_not(has_xm))
        def _(ref=ref):
            ref[:, 0:H, :] = jnp.zeros((ref.shape[0], H, ref.shape[2]), f32)

        @pl.when(jnp.logical_not(has_xp))
        def _(ref=ref, rows=rows):
            ref[:, rows - H:rows, :] = jnp.zeros((ref.shape[0], H, ref.shape[2]), f32)

    for ref in (UA, UB, UD, T1, M1, M2, M3, M4):
        planes = ref.shape[0]

        @pl.when(jnp.logical_not(has_ym))
        def _(ref=ref):
            ref[0] = jnp.zeros(ref.shape[1:], f32)

        @pl.when(jnp.logical_not(has_yp))
        def _(ref=ref, planes=planes):
            ref[planes - 1] = jnp.zeros(ref.shape[1:], f32)

    count = c_ref.shape[1]
    CB[...] = jnp.zeros(CB.shape, f32)
    CB[0, :, 0:count] = jnp.broadcast_to(c_ref[...], (8, count))

    barrier = pltpu.get_barrier_semaphore()
    for s in range(1, npx):
        pl.semaphore_signal(barrier, inc=1, device_id={"px": lax.rem(i + s, npx), "py": j}, device_id_type=MESH)
    for s in range(1, npy):
        pl.semaphore_signal(barrier, inc=1, device_id={"px": i, "py": lax.rem(j + s, npy)}, device_id_type=MESH)
    for to_x in (xm, xp):
        for to_y in (ym, yp):
            pl.semaphore_signal(barrier, inc=1, device_id={"px": to_x, "py": to_y}, device_id_type=MESH)

    pending = []

    def push(src, dst, to_x, to_y, sends=None, receives=None):
        at = len(pending)
        copy = pltpu.make_async_remote_copy(
            src_ref=src, dst_ref=dst, send_sem=ss.at[at], recv_sem=rs.at[at],
            device_id={"px": to_x, "py": to_y}, device_id_type=MESH,
        )
        if sends is None:
            copy.start()
        else:
            pl.when(sends)(copy.start)
        pending.append((sends, copy))
        return receives, copy

    def arrive(handles):
        for receives, copy in handles:
            if receives is None:
                copy.wait_recv()
            else:
                pl.when(receives)(copy.wait_recv)

    def sent(sends, copy):
        if sends is None:
            copy.wait_send()
        else:
            pl.when(sends)(copy.wait_send)

    def halo_x(ref, planes, rows, zs):
        a, b = planes
        return [
            push(ref.at[a:b, rows:rows + H, zs], ref.at[a:b, 0:H, zs], xp, j, has_xp, has_xm),
            push(ref.at[a:b, H:2 * H, zs], ref.at[a:b, rows + H:rows + 2 * H, zs], xm, j, has_xm, has_xp),
        ]

    def halo_y(ref, planes, r, zs):
        return [
            push(ref.at[planes, r, zs], ref.at[0, r, zs], i, yp, has_yp, has_ym),
            push(ref.at[1, r, zs], ref.at[planes + 1, r, zs], i, ym, has_ym, has_yp),
        ]

    def halo(ref, planes, rows, zs):
        return halo_y(ref, planes, slice(H, H + rows), zs) + halo_x(ref, (1, planes + 1), rows, zs)

    def halo_corners(ref, planes, rows, zs):
        both = jnp.logical_and
        low, high = slice(0, H), slice(rows + H, rows + 2 * H)
        first, last = slice(H, 2 * H), slice(rows, rows + H)
        return [
            push(ref.at[planes, last, zs], ref.at[0, low, zs], xp, yp, both(has_xp, has_yp), both(has_xm, has_ym)),
            push(ref.at[1, last, zs], ref.at[planes + 1, low, zs], xp, ym, both(has_xp, has_ym), both(has_xm, has_yp)),
            push(ref.at[planes, first, zs], ref.at[0, high, zs], xm, yp, both(has_xm, has_yp), both(has_xp, has_ym)),
            push(ref.at[1, first, zs], ref.at[planes + 1, high, zs], xm, ym, both(has_xm, has_ym), both(has_xp, has_yp)),
        ]

    def to_block(ref, at, rows, peers, zs):
        here = lax.rem(i, peers)
        base = i - here
        mine = ref.at[:, pl.ds(at, rows), zs]
        return [push(mine, mine, base + lax.rem(here + s, peers), j) for s in range(1, peers)]

    def residual(rhs, ref, rho, cx, cys, cz, y, k):
        rows = rhs.shape[1]
        lo = k * B
        zs = slice(lo, lo + B)
        own = slice(H, H + rows)
        c = ref[y + 1, own, zs]
        near_x = ref[y + 1, H - 1:H - 1 + rows, zs] + ref[y + 1, H + 1:H + 1 + rows, zs]
        near_y = ref[y, own, zs] + ref[y + 2, own, zs]
        blank = jnp.zeros((rows, 128), f32)
        left = ref[y + 1, own, lo - 128:lo] if lo > 0 else blank
        right = ref[y + 1, own, lo + B:lo + B + 128] if lo + B < ref.shape[2] else blank
        wide = jnp.concatenate([left, c, right], axis=1)
        near_z = (pltpu.roll(wide, 1, 1) + pltpu.roll(wide, B + 255, 1))[:, 128:128 + B]
        twice = 2.0 * c
        stencil = cx[...] * (twice - near_x) + cys[y] * (twice - near_y) + cz[0:1, zs] * (twice - near_z)
        return rhs[y, :, zs] - (shift_term * c + rho[y, :, zs] * stencil)

    def inverse_diagonal(rho, cx, cys, cz, y, k):
        zs = slice(k * B, k * B + B)
        return 1.0 / (shift_term + 2.0 * rho[y, :, zs] * (cx[...] + cys[y] + cz[0:1, zs]))

    square = (n, n)
    diag = lax.broadcasted_iota(jnp.int32, square, 0) == lax.broadcasted_iota(jnp.int32, square, 1)
    column = jnp.sum(jnp.where(diag, jnp.broadcast_to(sx_ref[...], square), 0.0), axis=1, keepdims=True)
    CX[...] = jnp.broadcast_to(column, (n, B))
    cy = [sy_ref[y] for y in range(ny)]
    cy1 = [(cy[2 * y] + cy[2 * y + 1]) * 0.125 for y in range(ny1)]

    neighbours = []

    def enter():
        pl.semaphore_wait(barrier, npx + npy + 2)
        neighbours.extend([
            push(CB.at[0], CB.at[1], xp, j, has_xp, has_xm),
            push(CB.at[0], CB.at[2], xm, j, has_xm, has_xp),
            push(CB.at[0], CB.at[3], i, yp, has_yp, has_ym),
            push(CB.at[0], CB.at[4], i, ym, has_ym, has_yp),
        ])

    def smooth_z(values, block, planes, rows):
        w = jnp.concatenate(values, axis=0)
        z = mm3(split(w), split(block), True)
        return [z[y * rows:(y + 1) * rows] for y in range(planes)]

    def window(ref, y, k, width, side):
        lo = k * width
        parts = [ref[y, :, lo:lo + width]]
        blank = jnp.zeros((ref.shape[1], side), f32)
        parts.insert(0, ref[y, :, lo - side:lo] if lo > 0 else blank)
        parts.append(ref[y, :, lo + width:lo + width + side] if lo + width < ref.shape[2] else blank)
        return jnp.concatenate(parts, axis=1)

    own = slice(H, H + n)
    own1 = slice(H, H + n1)
    mean_x = weights((n1, n), 1, 0, 0, 0.5, 0.0)
    mean_z = weights((B, half), 0, 0, 0, 0.5, 0.0)

    def scaled_residual(ref, halos, target, blocks, k):
        arrive(halos[k])
        for y in range(ny):
            r = residual(F, ref, RHO, CX, cy, sz_ref, y, k)
            target[y, pl.ds(at0, n), cols[k]] = r * RD[y, :, cols[k]]
        blocks.append(to_block(target, at0, n, g, cols[k]))

    halos, blocks = [], []
    for k in range(nk):
        if k == 0:
            for copy in first_loads:
                copy.wait()
        for tile in range(k * B // 128, (k + 1) * B // 128):
            for y in range(ny):
                F[y, :, tile * 128:tile * 128 + 128] = FS[rows_of(y, tile), :]
                RHO[y, :, tile * 128:tile * 128 + 128] = RS[rows_of(y, tile), :]
        scaled = []
        for y in range(ny):
            rd = inverse_diagonal(RHO, CX, cy, sz_ref, y, k)
            RD[y, :, cols[k]] = rd
            scaled.append(F[y, :, cols[k]] * rd)
        solved = smooth_z(scaled, LZ0[k], ny, n)
        for y in range(ny):
            UA[y + 1, own, cols[k]] = solved[y]
        if k == 0:
            enter()
        halos.append(halo(UA, ny, n, cols[k]))
    for k in range(nk):
        scaled_residual(UA, halos, W, blocks, k)

    for copy in late:
        copy.wait()
    restrict_x = weights((n1, n + 2 * H), 1, H, 0, 0.375, 0.125)
    restrict_z = weights((B + 256, half), 0, 128, 0, 0.375, 0.125)
    CX1[...] = left_mul(mean_x, CX[...]) * 0.25
    for k in range(nk):
        fine_z = jnp.broadcast_to(sz_ref[:, cols[k]], (8, B))
        CZ1[:, k * half:k * half + half] = right_mul(fine_z, mean_z) * 0.25
        for y in range(ny1):
            pair = (RHO[2 * y, :, cols[k]] + RHO[2 * y + 1, :, cols[k]]) * 0.5
            RHO1[y, :, k * half:k * half + half] = right_mul(left_mul(mean_x, pair), mean_z)
    for y in range(ny1):
        for k in range(nk1):
            RD1[y, :, cols[k]] = inverse_diagonal(RHO1, CX1, cy1, CZ1, y, k)

    lx0 = split(LX0[...])
    halos, rims, sides, halos1 = [], [], [], []

    def fine_residual(k):
        arrive(halos[k])
        for y in range(ny):
            R0[y, own, cols[k]] = residual(F, UB, RHO, CX, cy, sz_ref, y, k)
        rims.append(halo_x(R0, (0, ny), n, cols[k]))

    def restrict_rows(k):
        arrive(rims[k])
        for y in range(ny):
            TX[y, :, cols[k]] = left_mul(restrict_x, R0[y, :, cols[k]])

    def restrict_columns(k):
        zs = slice(k * half, k * half + half)
        for y in range(ny):
            T1[y + 1, :, zs] = right_mul(window(TX, y, k, B, 128), restrict_z)
        sides.append(halo_y(T1, ny, slice(None), zs))

    def middle_rhs(k):
        arrive(sides[2 * k])
        arrive(sides[2 * k + 1])
        for y in range(ny1):
            a = 2 * y
            inner = T1[a + 1, :, cols[k]] + T1[a + 2, :, cols[k]]
            F1[y, :, cols[k]] = (T1[a, :, cols[k]] + 3.0 * inner + T1[a + 3, :, cols[k]]) * 0.125

    def middle_z(ref, before, rhs, k):
        scaled = [r * RD1[y, :, cols[k]] for y, r in enumerate(rhs)]
        solved = smooth_z(scaled, LZ1[k], ny1, n1)
        for y in range(ny1):
            u = solved[y] if before is None else before[y + 1, own1, cols[k]] + solved[y]
            ref[y + 1, own1, cols[k]] = u
        return halo(ref, ny1, n1, cols[k])

    def middle_first(k):
        middle_rhs(k)
        halos1.append(middle_z(M1, None, [F1[y, :, cols[k]] for y in range(ny1)], k))

    for k in range(nk):
        arrive(blocks[k])
        for y in range(ny):
            UB[y + 1, own, cols[k]] = UA[y + 1, own, cols[k]] + mm3(lx0, split(W[y, :, cols[k]]))
        halos.append(halo(UB, ny, n, cols[k]))
    for k in range(nk):
        fine_residual(k)
    for k in range(nk):
        restrict_rows(k)
    for k in range(nk):
        restrict_columns(k)
    for k in range(nk1):
        middle_first(k)

    lx1 = split(LX1[...])

    def middle_x(ref, halos1, target, result, diagonals):
        sent = []
        for k in range(nk1):
            arrive(halos1[k])
            for y in range(ny1):
                r = residual(F1, ref, RHO1, CX1, cy1, CZ1, y, k)
                target[y, pl.ds(at1, n1), cols[k]] = r * RD1[y, :, cols[k]]
            sent.append(to_block(target, at1, n1, g1, cols[k]))
        edges = []
        for k in range(nk1):
            arrive(sent[k])
            for y in range(ny1):
                solved = mm3(lx1, split(target[y, :, cols[k]]))
                result[y + 1, own1, cols[k]] = ref[y + 1, own1, cols[k]] + solved
            edge = halo(result, ny1, n1, cols[k])
            if diagonals:
                edge = edge + halo_corners(result, ny1, n1, cols[k])
            edges.append(edge)
        return edges

    edges = middle_x(M1, halos1, V, M2, False)

    total = jnp.zeros((1, B), f32)
    for k in range(nk1):
        arrive(edges[k])
        for y in range(ny1):
            r = residual(F1, M2, RHO1, CX1, cy1, CZ1, y, k)
            total = total + jnp.sum(r, axis=0, keepdims=True)
    mean = jnp.sum(total, axis=1, keepdims=True) * (1.0 / (ny1 * n1 * nz1))
    lane = lax.broadcasted_iota(jnp.int32, CB.shape[1:], 1)
    G1[i] = jnp.where(lane == j * npx + i, mean, 0.0)
    arrive([push(G1.at[i], G1.at[i], lax.rem(i + s, npx), j) for s in range(1, npx)])
    G2[j] = jnp.sum(G1[...], axis=0)
    arrive([push(G2.at[j], G2.at[j], i, lax.rem(j + s, npy)) for s in range(1, npy)])
    means = jnp.sum(G2[...], axis=0)[0:1]
    arrive(neighbours)
    e = [jnp.sum(CB[s][0:1] * means, axis=1, keepdims=True) for s in range(5)]
    MP[1:ny1 + 1, own1, :] = M2[1:ny1 + 1, own1, :] + e[0]
    MP[1:ny1 + 1, 0:H, :] = M2[1:ny1 + 1, 0:H, :] + e[1]
    MP[1:ny1 + 1, n1 + H:n1 + 2 * H, :] = M2[1:ny1 + 1, n1 + H:n1 + 2 * H, :] + e[2]
    MP[0, own1, :] = M2[0, own1, :] + e[3]
    MP[ny1 + 1, own1, :] = M2[ny1 + 1, own1, :] + e[4]

    halos1 = []
    for k in range(nk1):
        rhs = [residual(F1, MP, RHO1, CX1, cy1, CZ1, y, k) for y in range(ny1)]
        halos1.append(middle_z(M3, MP, rhs, k))
    edges = middle_x(M3, halos1, V2, M4, True)

    raise_x = weights((n + 2 * H, n1 + 2 * H), 0, H, H, 0.75, 0.25)
    raise_z = weights((half + 256, B), 1, 0, 128, 0.75, 0.25)
    row = lax.broadcasted_iota(jnp.int32, (n + 2 * H, 1), 0)
    inside = jnp.logical_and(jnp.logical_or(row >= H, has_xm), jnp.logical_or(row < n + H, has_xp))
    arrived = []

    def prolong(k):
        while len(arrived) < min(k + 1, nk - 1) // 2 + 1:
            arrive(edges[len(arrived)])
            arrived.append(k)
        zs = cols[k]
        raised = [left_mul(raise_x, right_mul(window(M4, y, k, half, 128), raise_z)) for y in range(ny1 + 2)]
        for y in range(ny + 2):
            near = (y - 1) // 2 + 1
            other = near - 1 if (y - 1) % 2 == 0 else near + 1
            c = (3.0 * raised[near] + raised[other]) * 0.25
            if y == 0:
                UC[0, own, zs] = jnp.where(has_ym, UB[0, own, zs] + c[own], 0.0)
            elif y == ny + 1:
                UC[y, own, zs] = jnp.where(has_yp, UB[y, own, zs] + c[own], 0.0)
            else:
                UC[y, :, zs] = jnp.where(inside, UB[y, :, zs] + c, 0.0)

    settled = len(pending)
    halos, blocks = [], []
    prolong(0)
    for k in range(nk):
        if k + 1 < nk:
            prolong(k + 1)
        scaled = [residual(F, UC, RHO, CX, cy, sz_ref, y, k) * RD[y, :, cols[k]] for y in range(ny)]
        solved = smooth_z(scaled, LZ0[k], ny, n)
        for y in range(ny):
            UD[y + 1, own, cols[k]] = UC[y + 1, own, cols[k]] + solved[y]
        halos.append(halo(UD, ny, n, cols[k]))
    for k in range(nk):
        scaled_residual(UD, halos, W2, blocks, k)
    lx0 = split(LX0[...])
    for sends, copy in pending[:settled]:
        sent(sends, copy)
    for k in range(nk):
        arrive(blocks[k])
        for y in range(ny):
            result = UD[y + 1, own, cols[k]] + mm3(lx0, split(W2[y, :, cols[k]]))
            for t in range(B // 128):
                FS[rows_of(y, k * B // 128 + t), :] = result[:, t * 128:t * 128 + 128]
    store = pltpu.make_async_copy(FS, out_ref, ls.at[0])
    store.start()
    for sends, copy in pending[settled:]:
        sent(sends, copy)
    store.wait()


def per_device(npx, npy, f, rho, sx, sy, sz, lz0, lx0, lz1, lx1, c):
    n, ny, nz = f.shape
    B = lz0.shape[-1]
    n1, ny1, nz1 = n // 2, ny // 2, nz // 2
    g, g1, nk = B // n, B // n1, nz // B
    lanes = -(-c.shape[1] // 128) * 128
    linear = pltpu.VMEM((n * nz // 128 * ny, 128), f32)
    fine = pltpu.VMEM((ny, n, nz), f32)
    padded = pltpu.VMEM((ny + 2, n + 2 * H, nz), f32)
    coarse = pltpu.VMEM((ny1, n1, nz1), f32)
    coarse_padded = pltpu.VMEM((ny1 + 2, n1 + 2 * H, nz1), f32)
    copies = 4 + nk * (14 + 2 * g) + nk // 2 * (18 + 2 * g1) + npx + npy - 2

    def rows(field):
        return field.reshape(n, ny, nz // 128, 128).transpose(0, 2, 1, 3).reshape(-1, 128)

    anywhere = pl.BlockSpec(memory_space=pl.ANY)
    vmem = pl.BlockSpec(memory_space=pltpu.VMEM)
    smem = pl.BlockSpec(memory_space=pltpu.SMEM)
    out = pl.pallas_call(
        functools.partial(kernel, (n, ny, nz, B, npx, npy)),
        out_shape=jax.ShapeDtypeStruct((n * nz // 128 * ny, 128), f32),
        in_specs=[anywhere, anywhere, vmem, smem, vmem, anywhere, anywhere, anywhere, anywhere, vmem],
        out_specs=anywhere,
        scratch_shapes=[
            fine, fine, fine, padded, padded, padded, padded,
            pltpu.VMEM((ny, B, nz), f32), pltpu.VMEM((ny, B, nz), f32),
            pltpu.VMEM((ny, n + 2 * H, nz), f32), pltpu.VMEM((ny, n1, nz), f32), pltpu.VMEM((ny + 2, n1, nz1), f32),
            coarse, coarse, coarse,
            coarse_padded, coarse_padded, coarse_padded, coarse_padded, coarse_padded,
            pltpu.VMEM((ny1, B, nz1), f32), pltpu.VMEM((ny1, B, nz1), f32),
            pltpu.VMEM((npx, 8, lanes), f32), pltpu.VMEM((npy, 8, lanes), f32), pltpu.VMEM((5, 8, lanes), f32),
            pltpu.VMEM((n, B), f32), pltpu.VMEM((n1, B), f32), pltpu.VMEM((8, nz1), f32),
            pltpu.VMEM(lz0.shape, f32), pltpu.VMEM(lz1.shape, f32),
            pltpu.VMEM((n, B), f32), pltpu.VMEM((n1, B), f32), linear, linear,
            pltpu.SemaphoreType.DMA((copies,)), pltpu.SemaphoreType.DMA((copies,)),
            pltpu.SemaphoreType.DMA((6,)),
        ],
        compiler_params=pltpu.CompilerParams(
            collective_id=0, has_side_effects=True, vmem_limit_bytes=56 * 1024 * 1024
        ),
    )(rows(f), rows(rho), sx.reshape(1, n), sy, sz.reshape(1, nz), lz0, lx0, lz1, lx1, c)
    return out.reshape(n, nz // 128, ny, 128).transpose(0, 2, 1, 3).reshape(n, ny, nz)


def solution(mesh):
    placed = (
        P("px", "py", None), P("px", "py", None), P("px"), P("py"),
        P(), P(), P(), P(), P(), P(("py", "px"), None),
    )
    body = functools.partial(per_device, mesh.shape["px"], mesh.shape["py"])
    return jax.shard_map(
        body, mesh=mesh, in_specs=placed, out_specs=P("px", "py", None), check_vma=False
    )
```
